1024 devices in a mesh: dp: 32 (over y_hi, x, core), expert: 32 (over z, y_lo).
Axes of the slice: x: 8, y: 8 (y_hi: 2, y_lo: 4; y = y_hi * 4 + y_lo), z: 8, core: 2. Of those that a mesh axis runs over, the one named last changes fastest.
Arguments:
- grads: bfloat16 [32, 288, 57344], P('dp', 'expert'), may hold values from -6 to 6
- weights: bfloat16 [256, 57344], P('expert', 'dp'), may hold values from -3 to 3
- first: float32 [256, 57344], P('expert', 'dp'), may hold values from -3 to 3
- second: float32 [256, 57344], P('expert', 'dp'), may hold values from 0.25 to 1
- old_home: int32 [256], replicated, may hold values from 0 to 255, as said below
- old_extra: int32 [32], replicated, may hold values from 0 to 255, as said below
- new_home: int32 [256], replicated, may hold values from 0 to 255, as said below
- new_extra: int32 [32], replicated, may hold values from 0 to 255, as said below
Outputs:
- new_weights: bfloat16 [288, 57344], P('expert', 'dp')
- new_first: float32 [256, 57344], P('expert', 'dp')
- new_second: float32 [256, 57344], P('expert', 'dp')
The draws below stay inside these ranges and needn't reach their ends.
Inputs may be any that keep to these rules, and one draw needn't show every extreme that they name: `old_home`: A permutation of the expert ids. `new_home`: A permutation of the expert ids. Exactly one home slot of each expert device holds under new_home an expert whose old home slot lies on another expert device; the other home slots keep their experts. `old_extra`: expert ids; an expert may fill several redundant slots. `new_extra`: expert ids; an expert may fill several redundant slots.
All inputs are finite; a program needn't handle non-finite values.
Results may differ from the reference program's by a relative error of at most 0.0004.
Values may be sent and summed in bfloat16 or wider, within the bound.
No kernel may reach another device: no remote copies, remote signals or barrier semaphores. Data moves between devices by JAX's collectives and lax.ppermute only.
A program may use at most 32 MiB of HBM per device.

```python
import math
import jax
import jax.numpy as jnp
from jax import lax

EXP_DEV = 8
REP_DEV = 1
EXPERTS = 256
REDUND = 32
SLOTS = 288
PARAMS = 57344
GROUPS = 32
N_EXPERT = 32


def home_tables(key):
    key_perm = jax.random.fold_in(key, 11)
    key_order = jax.random.fold_in(key, 12)
    key_cols = jax.random.fold_in(key, 13)
    old_list = jax.random.permutation(key_perm, EXPERTS).astype(jnp.int32)
    order = jax.random.permutation(key_order, N_EXPERT).astype(jnp.int32)
    columns = jax.random.randint(key_cols, (N_EXPERT,), 0, EXP_DEV).astype(jnp.int32)
    src_slot = order * EXP_DEV + columns[order]
    dst_slot = jnp.roll(src_slot, -1)
    new_list = old_list.at[dst_slot].set(old_list[src_slot])
    return (old_list, new_list)


def extra_list(key):
    key_one = jax.random.fold_in(key, 21)
    key_two = jax.random.fold_in(key, 22)
    first_ids = jax.random.randint(key_one, (REDUND,), 0, EXPERTS)
    second_ids = jax.random.randint(key_two, (REDUND,), 0, EXPERTS)
    chosen = jnp.minimum(first_ids, second_ids).astype(jnp.int32)
    chosen = chosen.at[0].set(EXPERTS - 1).at[1].set(0)
    return chosen.astype(jnp.int32)


def draw_old_home(key, part):
    return home_tables(key)[0]


def draw_new_home(key, part):
    return home_tables(key)[1]


def draw_old_extra(key, part):
    key = jax.random.fold_in(key, 3)
    return extra_list(key)


def draw_new_extra(key, part):
    key = jax.random.fold_in(key, 4)
    return extra_list(key)


def strengthened(array, key, source, target, blocks, factor):
    def block_of(dim):
        return (jnp.arange(array.shape[dim]) // (array.shape[dim] // blocks)).reshape((-1,) + (1,) * (array.ndim - 1 - dim))

    first = jax.random.permutation(key, blocks)[block_of(target)]
    far = (block_of(target) + blocks // 2) % blocks
    return jnp.where((block_of(source) == first) | (block_of(source) == far), factor * array, array)


def steps_of(rng, extent, cuts, low, top_value):
    level, own = 1.0, jax.random.fold_in(rng, 6)
    for axis_at, shards_of in cuts:
        draws = jnp.exp(jax.random.uniform(jax.random.fold_in(own, axis_at), (shards_of,), jnp.float32, low / len(cuts), top_value / len(cuts)))
        level = level * jnp.repeat(draws, extent[axis_at] // shards_of).reshape([-1 if axis == axis_at else 1 for axis in range(len(extent))])
    return level


def normal_values(key, shape, scale, reach, cuts=(), held_as=jnp.bfloat16):
    factor_of = steps_of(key, shape, cuts, -0.22, 0.18) if cuts else 1.0
    entries = jax.random.normal(key, shape, jnp.float32) * scale * factor_of
    return jnp.minimum(jnp.maximum(entries, -reach), reach).astype(held_as)


def gaussian_with(own_key, dims, scale, most, pieces, heavy, dtype=jnp.bfloat16):
    result = scale * jax.random.normal(own_key, dims, jnp.float32)
    if pieces:
        result = result * steps_of(own_key, dims, pieces, -0.22, 0.18)
    return jnp.clip(strengthened(result, jax.random.fold_in(own_key, 3), *heavy), -most, most).astype(dtype)


def setup_inputs(seed: int = 0) -> dict:
    seeds = jax.random.split(jax.random.key(seed), 9)
    grads = gaussian_with(seeds[0], (GROUPS, SLOTS, PARAMS), 0.5, 6.0, ((0, 32), (1, 32)), (0, 2, 32, 2.75))
    weights = normal_values(seeds[1], (EXPERTS, PARAMS), 0.5, 3.0, ((0, 32), (1, 32)))
    first = normal_values(seeds[2], (EXPERTS, PARAMS), 0.3, 3.0, ((0, 32), (1, 32)), jnp.float32)
    second = jnp.clip(jnp.exp(math.log(1.0) - 1.3862944 * jax.random.uniform(seeds[3], (EXPERTS, PARAMS), jnp.float32) ** steps_of(seeds[3], (EXPERTS, PARAMS), ((0, 32), (1, 32)), -0.2, 0.2)), 0.25, 1.0)
    old_home = draw_old_home(jax.random.fold_in(seeds[8], 71), 0)
    old_extra = draw_old_extra(jax.random.fold_in(seeds[8], 71), 0)
    new_home = draw_new_home(jax.random.fold_in(seeds[8], 71), 0)
    new_extra = draw_new_extra(jax.random.fold_in(seeds[8], 71), 0)
    return {"grads": grads, "weights": weights, "first": first, "second": second, "old_home": old_home, "old_extra": old_extra, "new_home": new_home, "new_extra": new_extra}


bias_first = 0.9999734386011124
bias_second = 0.994079470779696

def reference(grads, weights, first, second, old_home, old_extra, new_home, new_extra):
    width = grads.shape[2]
    groups = grads.shape[0]

    def add_group(g, acc):
        part = lax.dynamic_index_in_dim(grads, g, 0, keepdims=False).astype(jnp.float32)
        return acc + part
    summed = lax.fori_loop(0, groups, add_group, jnp.zeros((grads.shape[1], width), jnp.float32))
    summed = summed.reshape(N_EXPERT, EXP_DEV + REP_DEV, width)
    home_grad = summed[:, :EXP_DEV].reshape(N_EXPERT * EXP_DEV, width)
    extra_grad = summed[:, EXP_DEV:].reshape(N_EXPERT * REP_DEV, width)
    match = (old_home[:, None] == old_extra[None, :]).astype(jnp.float32)
    total = home_grad + jnp.dot(match, extra_grad, precision=lax.Precision.HIGHEST)
    moment1 = 0.9 * first + 0.1 * total
    moment2 = 0.95 * second + 0.05 * total * total
    base = weights.astype(jnp.float32)
    step = moment1 / bias_first / (jnp.sqrt(moment2 / bias_second) + 1e-08)
    updated = (base - 0.02 * (step + 0.1 * base)).astype(jnp.bfloat16)
    inverse = jnp.argsort(old_home).astype(jnp.int32)
    source = inverse[new_home]
    extra_source = inverse[new_extra]
    new_first = moment1[source]
    new_second = moment2[source]
    home_part = updated[source].reshape(N_EXPERT, EXP_DEV, width)
    extra_part = updated[extra_source].reshape(N_EXPERT, REP_DEV, width)
    new_weights = jnp.concatenate([home_part, extra_part], axis=1).reshape(-1, width)
    return (new_weights, new_first, new_second)
```

```python
import jax
import jax.numpy as jnp
from jax import lax
from jax.experimental import pallas as pl
from jax.experimental.pallas import tpu as pltpu
from jax.sharding import Mesh
from jax.sharding import PartitionSpec as P

bias_first = 0.9999734386011124
bias_second = 0.994079470779696
LANES = 128
ROW = 16
PAIR_SCALE = 4096.0
SUM_SCALE = 256.0
STATE_SCALE = 16384.0

F32 = jnp.float32
F16 = jnp.float16
BF16 = jnp.bfloat16
VMEM = pl.BlockSpec(memory_space=pltpu.VMEM)
SMEM = pl.BlockSpec(memory_space=pltpu.SMEM)


def cost(n):
    return pl.CostEstimate(flops=n, bytes_accessed=4 * n, transcendentals=0)


def split_kernel(homes, width, steps, grads_ref, out_ref, line):
    tiles = width // LANES
    line[...] = jnp.zeros_like(line)
    for j in range(steps):
        for c in range(2):
            at = (2 * j + c) * width
            block = grads_ref[0, :, at : at + width].astype(F32)
            for t in range(0, tiles, 2):
                low = block[:homes, t * LANES : (t + 1) * LANES]
                high = block[:homes, (t + 1) * LANES : (t + 2) * LANES]
                out_ref[c, j, t * homes : (t + 2) * homes, :] = jnp.concatenate([low, high], axis=0).astype(BF16)
            for t in range(tiles):
                line[t : t + 1, :] = block[homes : homes + 1, t * LANES : (t + 1) * LANES]
            out_ref[c, j, tiles * homes : tiles * homes + ROW, :] = line[...].astype(BF16)


def split_by_core(grads, outer, width):
    homes = grads.shape[1] - 1
    rows = (width // LANES) * homes + ROW
    steps = 4 if outer % 4 == 0 else 1
    return pl.pallas_call(
        lambda *refs: split_kernel(homes, width, steps, *refs),
        grid=(outer // steps,),
        in_specs=[pl.BlockSpec((1, homes + 1, steps * 2 * width), lambda i: (0, 0, i))],
        out_specs=pl.BlockSpec((2, steps, rows, LANES), lambda i: (0, i, 0, 0)),
        out_shape=jax.ShapeDtypeStruct((2, outer, rows, LANES), BF16),
        scratch_shapes=[pltpu.VMEM((ROW, LANES), F32)],
        compiler_params=pltpu.CompilerParams(vmem_limit_bytes=16 * 2**20),
        cost_estimate=cost(1 << 19),
    )(grads)


def state_kernel(scal, w_ref, f_ref, s_ref, out_ref, rows):
    homes, width = f_ref.shape
    tiles = width // LANES
    rows[...] = jnp.zeros_like(rows)
    for n, ref in enumerate((w_ref, f_ref, s_ref)):
        value = ref[...].astype(F32) * STATE_SCALE
        for i in range(homes):
            for t in range(tiles):
                rows[i, n * ROW + t : n * ROW + t + 1, :] = value[i : i + 1, t * LANES : (t + 1) * LANES]
    leaving = rows[scal[0]]
    for d in range(out_ref.shape[0]):
        out_ref[d, : 3 * ROW, :] = leaving
        out_ref[d, 3 * ROW :, :] = rows[scal[8 + d]]


def sums_kernel(scal, s_ref, out_ref, rows):
    homes = rows.shape[0]
    tiles = (s_ref.shape[0] - ROW) // homes
    rows[...] = jnp.zeros_like(rows)
    for i in range(homes):
        for t in range(tiles):
            rows[i, t : t + 1, :] = s_ref[t * homes + i : t * homes + i + 1, :]
    extra = s_ref[tiles * homes :, :]
    leaving = rows[scal[0]]
    for d in range(out_ref.shape[0]):
        out_ref[d, :ROW, :] = extra
        out_ref[d, ROW : 2 * ROW, :] = leaving
        out_ref[d, 2 * ROW :, :] = rows[scal[8 + d]]


def adam(total, base, first, second):
    moment1 = 0.9 * first + 0.1 * total
    moment2 = 0.95 * second + 0.05 * total * total
    step = moment1 / bias_first / (jnp.sqrt(moment2 / bias_second) + 1e-08)
    return base - 0.02 * (step + 0.1 * base), moment1, moment2


def final_kernel(scal, sums_ref, late_ref, early_ref, w_ref, f_ref, s_ref, nw_ref, nf_ref, ns_ref, acc, flat):
    homes, width = f_ref.shape
    tiles = width // LANES
    devices = late_ref.shape[0]
    slot = scal[0]
    acc[...] = jnp.zeros_like(acc)
    acc[slot] = late_ref[scal[1], ROW : 2 * ROW, :]
    acc[homes] = late_ref[scal[2], 2 * ROW :, :]
    for s in range(devices):
        to = scal[8 + devices + s]

        @pl.when(to >= 0)
        def _():
            acc[to] += late_ref[s, :ROW, :]

        @pl.when(scal[8 + 2 * devices + s] > 0)
        def _():
            acc[homes] += late_ref[s, :ROW, :]

    for t in range(tiles):
        for i in range(homes + 1):
            flat[i : i + 1, t * LANES : (t + 1) * LANES] = acc[i, t : t + 1, :]
    is_new = lax.broadcasted_iota(jnp.int32, (homes, LANES), 0) == slot
    for t in range(tiles):
        cols = slice(t * LANES, (t + 1) * LANES)
        total = flat[:homes, cols] + jnp.where(is_new, 0.0, sums_ref[t * homes : (t + 1) * homes, :])
        base = jnp.where(is_new, early_ref[0:1, cols], w_ref[:, cols].astype(F32))
        first = jnp.where(is_new, early_ref[1:2, cols], f_ref[:, cols])
        second = jnp.where(is_new, early_ref[2:3, cols], s_ref[:, cols])
        updated, moment1, moment2 = adam(total, base, first, second)
        extra, _, _ = adam(flat[homes : homes + 1, cols], early_ref[3:4, cols], early_ref[4:5, cols], early_ref[5:6, cols])
        nf_ref[:, cols] = moment1
        ns_ref[:, cols] = moment2
        nw_ref[:, cols] = jnp.concatenate([updated, extra], axis=0).astype(BF16)


def routes(homes, old_home, old_extra, new_home, new_extra):
    me = lax.axis_index("expert")
    my_old = lax.dynamic_slice_in_dim(old_home, me * homes, homes)
    my_new = lax.dynamic_slice_in_dim(new_home, me * homes, homes)
    wanted = lax.dynamic_slice_in_dim(new_extra, me, 1)
    ids = jnp.arange(homes, dtype=jnp.int32)
    changed = my_old != my_new
    slot = jnp.sum(jnp.where(changed, ids, 0))
    arriving = jnp.sum(jnp.where(changed, my_new, 0))
    owner = jnp.arange(old_home.shape[0], dtype=jnp.int32) // homes
    source = jnp.sum(jnp.where(old_home == arriving, owner, 0))
    extra_source = jnp.sum(jnp.where(old_home == wanted, owner, 0))
    asked = jnp.sum(jnp.where(new_extra[:, None] == my_old[None, :], ids[None, :], 0), axis=1)
    adds = jnp.sum(jnp.where(old_extra[:, None] == my_new[None, :], ids[None, :] + 1, 0), axis=1) - 1
    extra_adds = (old_extra == wanted).astype(jnp.int32)
    head = jnp.stack([slot, source, extra_source] + [slot] * 5)
    return jnp.concatenate([head, asked, adds, extra_adds])


def per_device(grads, weights, first, second, old_home, old_extra, new_home, new_extra):
    homes, width = weights.shape
    tiles = width // LANES
    outer = lax.axis_size("outer")
    devices = lax.axis_size("expert")
    scal = routes(homes, old_home, old_extra, new_home, new_extra)
    states = pl.pallas_call(
        state_kernel,
        in_specs=[SMEM, VMEM, VMEM, VMEM],
        out_specs=VMEM,
        out_shape=jax.ShapeDtypeStruct((devices, 6 * ROW, LANES), F32),
        scratch_shapes=[pltpu.VMEM((homes, 3 * ROW, LANES), F32)],
        compiler_params=pltpu.CompilerParams(vmem_limit_bytes=16 * 2**20),
        cost_estimate=cost(1 << 18),
    )(scal, weights, first, second)
    early = lax.all_to_all(states.astype(F16), "expert", 0, 0, tiled=True)
    halves = split_by_core(grads, outer, width)
    pair = lax.all_to_all(halves, "core", 0, 0, tiled=True).astype(F32)
    partial = ((pair[0] + pair[1]) * PAIR_SCALE).astype(F16)
    parts = lax.all_to_all(partial, "outer", 0, 0, tiled=True)
    sums = jnp.sum(parts.astype(F32), axis=0) * (1.0 / PAIR_SCALE)
    outgoing = pl.pallas_call(
        sums_kernel,
        in_specs=[SMEM, VMEM],
        out_specs=VMEM,
        out_shape=jax.ShapeDtypeStruct((devices, 3 * ROW, LANES), F32),
        scratch_shapes=[pltpu.VMEM((homes, ROW, LANES), F32)],
        compiler_params=pltpu.CompilerParams(vmem_limit_bytes=16 * 2**20),
        cost_estimate=cost(1 << 18),
    )(scal, sums)
    late = lax.all_to_all((outgoing * SUM_SCALE).astype(F16), "expert", 0, 0, tiled=True)
    late = late.astype(F32) * (1.0 / SUM_SCALE)
    moved = lax.dynamic_slice(early, (scal[1], 0, 0), (1, 3 * ROW, LANES))
    copied = lax.dynamic_slice(early, (scal[2], 3 * ROW, 0), (1, 3 * ROW, LANES))
    state = jnp.concatenate([moved, copied], axis=1).astype(F32) * (1.0 / STATE_SCALE)
    state = state.reshape(6, ROW, LANES)[:, :tiles, :].reshape(6, width)
    return pl.pallas_call(
        final_kernel,
        in_specs=[SMEM] + [VMEM] * 6,
        out_specs=[VMEM] * 3,
        out_shape=[
            jax.ShapeDtypeStruct((homes + 1, width), BF16),
            jax.ShapeDtypeStruct((homes, width), F32),
            jax.ShapeDtypeStruct((homes, width), F32),
        ],
        scratch_shapes=[pltpu.VMEM((homes + 1, ROW, LANES), F32), pltpu.VMEM((ROW, width), F32)],
        compiler_params=pltpu.CompilerParams(vmem_limit_bytes=16 * 2**20),
        cost_estimate=cost(1 << 18),
    )(scal, sums, late, state, weights, first, second)


def solution(mesh):
    groups, devices = mesh.devices.shape
    grid = Mesh(mesh.devices.reshape(groups // 2, 2, devices), ("outer", "core", "expert"))
    dp = ("outer", "core")
    placed = (P(dp, "expert", None), P("expert", dp), P("expert", dp), P("expert", dp), P(), P(), P(), P())
    return jax.shard_map(
        per_device,
        mesh=grid,
        in_specs=placed,
        out_specs=(P("expert", dp), P("expert", dp), P("expert", dp)),
        check_vma=False,
    )
```

```python
import jax
import jax.numpy as jnp
from jax import lax
from jax.experimental import pallas as pl
from jax.experimental.pallas import tpu as pltpu
from jax.sharding import Mesh
from jax.sharding import PartitionSpec as P

bias_first = 0.9999734386011124
bias_second = 0.994079470779696
LANES = 128
ROW = 16
PAIR_SCALE = 4096.0
SUM_SCALE = 256.0
STATE_SCALE = 16384.0

F32 = jnp.float32
F16 = jnp.float16
BF16 = jnp.bfloat16
VMEM = pl.BlockSpec(memory_space=pltpu.VMEM)
SMEM = pl.BlockSpec(memory_space=pltpu.SMEM)


def cost(n):
    return pl.CostEstimate(flops=n, bytes_accessed=4 * n, transcendentals=0)


def split_kernel(homes, width, steps, grads_ref, out_ref, line):
    tiles = width // LANES
    line[...] = jnp.zeros_like(line)
    for j in range(steps):
        for c in range(2):
            at = (2 * j + c) * width
            block = grads_ref[0, :, at : at + width].astype(F32)
            for t in range(0, tiles, 2):
                low = block[:homes, t * LANES : (t + 1) * LANES]
                high = block[:homes, (t + 1) * LANES : (t + 2) * LANES]
                out_ref[c, j, t * homes : (t + 2) * homes, :] = jnp.concatenate([low, high], axis=0).astype(BF16)
            for t in range(tiles):
                line[t : t + 1, :] = block[homes : homes + 1, t * LANES : (t + 1) * LANES]
            out_ref[c, j, tiles * homes : tiles * homes + ROW, :] = line[...].astype(BF16)


def split_by_core(grads, outer, width):
    homes = grads.shape[1] - 1
    rows = (width // LANES) * homes + ROW
    steps = 4 if outer % 4 == 0 else 1
    return pl.pallas_call(
        lambda *refs: split_kernel(homes, width, steps, *refs),
        grid=(outer // steps,),
        in_specs=[pl.BlockSpec((1, homes + 1, steps * 2 * width), lambda i: (0, 0, i))],
        out_specs=pl.BlockSpec((2, steps, rows, LANES), lambda i: (0, i, 0, 0)),
        out_shape=jax.ShapeDtypeStruct((2, outer, rows, LANES), BF16),
        scratch_shapes=[pltpu.VMEM((ROW, LANES), F32)],
        compiler_params=pltpu.CompilerParams(vmem_limit_bytes=16 * 2**20),
        cost_estimate=cost(1 << 19),
    )(grads)


def rows_kernel(scal, sums_ref, w_ref, f_ref, s_ref, out_ref, rows):
    homes, width = f_ref.shape
    tiles = width // LANES
    for n, ref in enumerate((w_ref, f_ref, s_ref)):
        value = ref[...].astype(F32) * STATE_SCALE
        for i in range(homes):
            for t in range(tiles):
                at = n * tiles + t
                rows[i, at : at + 1, :] = value[i : i + 1, t * LANES : (t + 1) * LANES]
    sums = sums_ref[...] * SUM_SCALE
    for i in range(homes):
        for t in range(tiles):
            at = 3 * tiles + t
            rows[i, at : at + 1, :] = sums[t * homes + i : t * homes + i + 1, :]
    extra = sums[tiles * homes :, :]
    leaving = rows[scal[0]]
    per = 4 * tiles
    for d in range(out_ref.shape[0]):
        out_ref[d, :per, :] = leaving
        out_ref[d, per : 2 * per, :] = rows[scal[8 + d]]
        out_ref[d, 2 * per :, :] = extra


def adam(total, base, first, second):
    moment1 = 0.9 * first + 0.1 * total
    moment2 = 0.95 * second + 0.05 * total * total
    step = moment1 / bias_first / (jnp.sqrt(moment2 / bias_second) + 1e-08)
    return base - 0.02 * (step + 0.1 * base), moment1, moment2


def final_kernel(scal, sums_ref, extras_ref, got_ref, w_ref, f_ref, s_ref, nw_ref, nf_ref, ns_ref, acc, flat):
    homes, width = f_ref.shape
    tiles = width // LANES
    devices = extras_ref.shape[0]
    slot = scal[0]
    acc[...] = jnp.zeros_like(acc)
    for s in range(devices):
        to = scal[8 + devices + s]

        @pl.when(to >= 0)
        def _():
            acc[to] += extras_ref[s]

        @pl.when(scal[8 + 2 * devices + s] > 0)
        def _():
            acc[homes] += extras_ref[s]

    for t in range(tiles):
        cols = slice(t * LANES, (t + 1) * LANES)
        for i in range(homes + 1):
            flat[i : i + 1, cols] = acc[i, t : t + 1, :]
        for n in range(8):
            at = n * tiles + t
            flat[2 * homes + n : 2 * homes + n + 1, cols] = got_ref[at : at + 1, :]
    is_new = lax.broadcasted_iota(jnp.int32, (homes, LANES), 0) == slot
    for t in range(tiles):
        cols = slice(t * LANES, (t + 1) * LANES)
        got = flat[2 * homes : 2 * homes + 8, cols]
        own = sums_ref[t * homes : (t + 1) * homes, :]
        total = (flat[:homes, cols] + jnp.where(is_new, got[3:4], own * SUM_SCALE)) * (1.0 / SUM_SCALE)
        base = jnp.where(is_new, got[0:1] * (1.0 / STATE_SCALE), w_ref[:, cols].astype(F32))
        first = jnp.where(is_new, got[1:2] * (1.0 / STATE_SCALE), f_ref[:, cols])
        second = jnp.where(is_new, got[2:3] * (1.0 / STATE_SCALE), s_ref[:, cols])
        updated, moment1, moment2 = adam(total, base, first, second)
        total = (flat[homes : homes + 1, cols] + got[7:8]) * (1.0 / SUM_SCALE)
        state = got * (1.0 / STATE_SCALE)
        extra, _, _ = adam(total, state[4:5], state[5:6], state[6:7])
        nf_ref[:, cols] = moment1
        ns_ref[:, cols] = moment2
        nw_ref[:, cols] = jnp.concatenate([updated, extra], axis=0).astype(BF16)


def routes(homes, old_home, old_extra, new_home, new_extra):
    me = lax.axis_index("expert")
    my_old = lax.dynamic_slice_in_dim(old_home, me * homes, homes)
    my_new = lax.dynamic_slice_in_dim(new_home, me * homes, homes)
    wanted = lax.dynamic_slice_in_dim(new_extra, me, 1)
    ids = jnp.arange(homes, dtype=jnp.int32)
    changed = my_old != my_new
    slot = jnp.sum(jnp.where(changed, ids, 0))
    arriving = jnp.sum(jnp.where(changed, my_new, 0))
    owner = jnp.arange(old_home.shape[0], dtype=jnp.int32) // homes
    source = jnp.sum(jnp.where(old_home == arriving, owner, 0))
    extra_source = jnp.sum(jnp.where(old_home == wanted, owner, 0))
    asked = jnp.sum(jnp.where(new_extra[:, None] == my_old[None, :], ids[None, :], 0), axis=1)
    adds = jnp.sum(jnp.where(old_extra[:, None] == my_new[None, :], ids[None, :] + 1, 0), axis=1) - 1
    extra_adds = (old_extra == wanted).astype(jnp.int32)
    head = jnp.stack([slot, source, extra_source] + [slot] * 5)
    return jnp.concatenate([head, asked, adds, extra_adds])


def per_device(grads, weights, first, second, old_home, old_extra, new_home, new_extra):
    homes, width = weights.shape
    tiles = width // LANES
    outer = lax.axis_size("outer")
    devices = lax.axis_size("expert")
    scal = routes(homes, old_home, old_extra, new_home, new_extra)
    halves = split_by_core(grads, outer, width)
    pair = lax.all_to_all(halves, "core", 0, 0, tiled=True).astype(F32)
    partial = ((pair[0] + pair[1]) * PAIR_SCALE).astype(F16)
    parts = lax.all_to_all(partial, "outer", 0, 0, tiled=True)
    sums = jnp.sum(parts.astype(F32), axis=0) * (1.0 / PAIR_SCALE)
    outgoing = pl.pallas_call(
        rows_kernel,
        in_specs=[SMEM] + [VMEM] * 4,
        out_specs=VMEM,
        out_shape=jax.ShapeDtypeStruct((devices, 8 * tiles + ROW, LANES), F32),
        scratch_shapes=[pltpu.VMEM((homes, 4 * tiles, LANES), F32)],
        compiler_params=pltpu.CompilerParams(vmem_limit_bytes=16 * 2**20),
        cost_estimate=cost(1 << 18),
    )(scal, sums, weights, first, second)
    arrived = lax.all_to_all(outgoing.astype(F16), "expert", 0, 0, tiled=True)
    extras = arrived[:, 8 * tiles :, :].astype(F32)
    moved = lax.dynamic_slice(arrived, (scal[1], 0, 0), (1, 4 * tiles, LANES))
    copied = lax.dynamic_slice(arrived, (scal[2], 4 * tiles, 0), (1, 4 * tiles, LANES))
    got = jnp.concatenate([moved[0], copied[0]], axis=0).astype(F32)
    return pl.pallas_call(
        final_kernel,
        in_specs=[SMEM] + [VMEM] * 6,
        out_specs=[VMEM] * 3,
        out_shape=[
            jax.ShapeDtypeStruct((homes + 1, width), BF16),
            jax.ShapeDtypeStruct((homes, width), F32),
            jax.ShapeDtypeStruct((homes, width), F32),
        ],
        scratch_shapes=[pltpu.VMEM((homes + 1, ROW, LANES), F32), pltpu.VMEM((3 * homes, width), F32)],
        compiler_params=pltpu.CompilerParams(vmem_limit_bytes=16 * 2**20),
        cost_estimate=cost(1 << 18),
    )(scal, sums, extras, got, weights, first, second)


def solution(mesh):
    groups, devices = mesh.devices.shape
    grid = Mesh(mesh.devices.reshape(groups // 2, 2, devices), ("outer", "core", "expert"))
    dp = ("outer", "core")
    placed = (P(dp, "expert", None), P("expert", dp), P("expert", dp), P("expert", dp), P(), P(), P(), P())
    return jax.shard_map(
        per_device,
        mesh=grid,
        in_specs=placed,
        out_specs=(P("expert", dp), P("expert", dp), P("expert", dp)),
        check_vma=False,
    )
```

```python
import jax
import jax.numpy as jnp
from jax import lax
from jax.experimental import pallas as pl
from jax.experimental.pallas import tpu as pltpu
from jax.sharding import Mesh
from jax.sharding import PartitionSpec as P

bias_first = 0.9999734386011124
bias_second = 0.994079470779696
LANES = 128
ROW = 16
PAIR_SCALE = 4096.0
SUM_SCALE = 256.0
STATE_SCALE = 16384.0

F32 = jnp.float32
F16 = jnp.float16
BF16 = jnp.bfloat16
VMEM = pl.BlockSpec(memory_space=pltpu.VMEM)
SMEM = pl.BlockSpec(memory_space=pltpu.SMEM)


def cost(n):
    return pl.CostEstimate(flops=n, bytes_accessed=4 * n, transcendentals=0)


def split_kernel(homes, width, steps, grads_ref, out_ref, line):
    tiles = width // LANES
    line[...] = jnp.zeros_like(line)
    for j in range(steps):
        for c in range(2):
            at = (2 * j + c) * width
            block = grads_ref[0, :, at : at + width].astype(F32)
            for t in range(0, tiles, 2):
                low = block[:homes, t * LANES : (t + 1) * LANES]
                high = block[:homes, (t + 1) * LANES : (t + 2) * LANES]
                out_ref[c, j, t * homes : (t + 2) * homes, :] = jnp.concatenate([low, high], axis=0).astype(BF16)
            for t in range(tiles):
                line[t : t + 1, :] = block[homes : homes + 1, t * LANES : (t + 1) * LANES]
            out_ref[c, j, tiles * homes : tiles * homes + ROW, :] = line[...].astype(BF16)


def split_by_core(grads, outer, width):
    homes = grads.shape[1] - 1
    rows = (width // LANES) * homes + ROW
    steps = 4 if outer % 4 == 0 else 1
    return pl.pallas_call(
        lambda *refs: split_kernel(homes, width, steps, *refs),
        grid=(outer // steps,),
        in_specs=[pl.BlockSpec((1, homes + 1, steps * 2 * width), lambda i: (0, 0, i))],
        out_specs=pl.BlockSpec((2, steps, rows, LANES), lambda i: (0, i, 0, 0)),
        out_shape=jax.ShapeDtypeStruct((2, outer, rows, LANES), BF16),
        scratch_shapes=[pltpu.VMEM((ROW, LANES), F32)],
        compiler_params=pltpu.CompilerParams(vmem_limit_bytes=16 * 2**20),
        cost_estimate=cost(1 << 19),
    )(grads)


def leaving_kernel(slot_ref, w_ref, f_ref, s_ref, out_ref, wide):
    tiles = w_ref.shape[1] // LANES
    wide[...] = w_ref[...].astype(F32)
    out_ref[...] = jnp.zeros_like(out_ref)
    is_slot = lax.broadcasted_iota(jnp.int32, wide.shape, 0) == slot_ref[0]
    for n, ref in enumerate((wide, f_ref, s_ref)):
        row = jnp.sum(jnp.where(is_slot, ref[...], 0.0), axis=0, keepdims=True) * STATE_SCALE
        for t in range(tiles):
            out_ref[n * tiles + t : n * tiles + t + 1, :] = row[:, t * LANES : (t + 1) * LANES]


def rows_kernel(slot_ref, asked_ref, sums_ref, w_ref, f_ref, s_ref, out_ref, rows):
    homes, width = f_ref.shape
    tiles = width // LANES
    for n, ref in enumerate((w_ref, f_ref, s_ref)):
        value = ref[...].astype(F32) * STATE_SCALE
        for i in range(homes):
            for t in range(tiles):
                at = n * tiles + t
                rows[i, at : at + 1, :] = value[i : i + 1, t * LANES : (t + 1) * LANES]
    sums = sums_ref[...] * SUM_SCALE
    for i in range(homes):
        for t in range(tiles):
            at = 3 * tiles + t
            rows[i, at : at + 1, :] = sums[t * homes + i : t * homes + i + 1, :]
    extra = sums[tiles * homes :, :]
    slot = slot_ref[0]
    per = 4 * tiles
    rows[homes] = jnp.zeros_like(rows[homes])
    rows[homes, :tiles, :] = rows[slot, 3 * tiles :, :]
    leaving = rows[homes, :ROW, :]
    for d in range(out_ref.shape[0]):
        out_ref[d, :per, :] = rows[asked_ref[d]]
        out_ref[d, per : per + ROW, :] = extra
        out_ref[d, per + ROW :, :] = leaving


def adam(total, base, first, second):
    moment1 = 0.9 * first + 0.1 * total
    moment2 = 0.95 * second + 0.05 * total * total
    step = moment1 / bias_first / (jnp.sqrt(moment2 / bias_second) + 1e-08)
    return base - 0.02 * (step + 0.1 * base), moment1, moment2


def final_kernel(
    slot_ref, adds_ref, extra_adds_ref, sums_ref, extras_ref, got_ref, w_ref, f_ref, s_ref, nw_ref, nf_ref, ns_ref, acc, flat
):
    homes, width = f_ref.shape
    tiles = width // LANES
    slot = slot_ref[0]
    acc[...] = jnp.zeros_like(acc)
    for s in range(extras_ref.shape[0]):
        to = adds_ref[s]

        @pl.when(to >= 0)
        def _():
            acc[to] += extras_ref[s]

        @pl.when(extra_adds_ref[s] > 0)
        def _():
            acc[homes] += extras_ref[s]

    for t in range(tiles):
        cols = slice(t * LANES, (t + 1) * LANES)
        for i in range(homes + 1):
            flat[i : i + 1, cols] = acc[i, t : t + 1, :]
        for n in range(8):
            at = n * tiles + t
            flat[2 * homes + n : 2 * homes + n + 1, cols] = got_ref[at : at + 1, :]
    is_new = lax.broadcasted_iota(jnp.int32, (homes, LANES), 0) == slot
    for t in range(tiles):
        cols = slice(t * LANES, (t + 1) * LANES)
        got = flat[2 * homes : 2 * homes + 8, cols]
        own = sums_ref[t * homes : (t + 1) * homes, :]
        total = (flat[:homes, cols] + jnp.where(is_new, got[3:4], own * SUM_SCALE)) * (1.0 / SUM_SCALE)
        base = jnp.where(is_new, got[0:1] * (1.0 / STATE_SCALE), w_ref[:, cols].astype(F32))
        first = jnp.where(is_new, got[1:2] * (1.0 / STATE_SCALE), f_ref[:, cols])
        second = jnp.where(is_new, got[2:3] * (1.0 / STATE_SCALE), s_ref[:, cols])
        updated, moment1, moment2 = adam(total, base, first, second)
        total = (flat[homes : homes + 1, cols] + got[7:8]) * (1.0 / SUM_SCALE)
        state = got * (1.0 / STATE_SCALE)
        extra, _, _ = adam(total, state[4:5], state[5:6], state[6:7])
        nf_ref[:, cols] = moment1
        ns_ref[:, cols] = moment2
        nw_ref[:, cols] = jnp.concatenate([updated, extra], axis=0).astype(BF16)


def routes(homes, old_home, old_extra, new_home, new_extra):
    me = lax.axis_index("expert")
    my_old = lax.dynamic_slice_in_dim(old_home, me * homes, homes)
    my_new = lax.dynamic_slice_in_dim(new_home, me * homes, homes)
    wanted = lax.dynamic_slice_in_dim(new_extra, me, 1)
    ids = jnp.arange(homes, dtype=jnp.int32)
    changed = my_old != my_new
    slot = jnp.sum(jnp.where(changed, ids, 0))
    arriving = jnp.sum(jnp.where(changed, my_new, 0))
    owner = jnp.arange(old_home.shape[0], dtype=jnp.int32) // homes
    source = jnp.sum(jnp.where(old_home == arriving, owner, 0))
    extra_source = jnp.sum(jnp.where(old_home == wanted, owner, 0))
    asked = jnp.sum(jnp.where(new_extra[:, None] == my_old[None, :], ids[None, :], 0), axis=1)
    adds = jnp.sum(jnp.where(old_extra[:, None] == my_new[None, :], ids[None, :] + 1, 0), axis=1) - 1
    extra_adds = (old_extra == wanted).astype(jnp.int32)
    return slot, source, extra_source, asked, adds, extra_adds


def gather_leaving(row):
    devices = lax.axis_size("expert")
    me = lax.axis_index("expert")
    bits = [1 << k for k in range(devices.bit_length() - 1)]
    if len(bits) == 5:
        bits = [bits[k] for k in (4, 3, 1, 0, 2)]
    held = row[None]
    for bit in bits:
        other = lax.ppermute(held, "expert", [(i, i ^ bit) for i in range(devices)])
        held = jnp.concatenate([held, other], axis=0)

    def place(source):
        apart = jnp.bitwise_xor(source, me)
        return sum(jnp.where(jnp.bitwise_and(apart, bit) != 0, 1 << k, 0) for k, bit in enumerate(bits))

    return held, place


def per_device(grads, weights, first, second, old_home, old_extra, new_home, new_extra):
    homes, width = weights.shape
    tiles = width // LANES
    outer = lax.axis_size("outer")
    devices = lax.axis_size("expert")
    slot, source, extra_source, asked, adds, extra_adds = routes(homes, old_home, old_extra, new_home, new_extra)
    slot = slot.reshape(1)
    leaving = pl.pallas_call(
        leaving_kernel,
        in_specs=[SMEM] + [VMEM] * 3,
        out_specs=VMEM,
        out_shape=jax.ShapeDtypeStruct((3 * ROW, LANES), F32),
        scratch_shapes=[pltpu.VMEM((homes, width), F32)],
        compiler_params=pltpu.CompilerParams(vmem_limit_bytes=16 * 2**20),
        cost_estimate=cost(1 << 16),
    )(slot, weights, first, second)
    held, place = gather_leaving(leaving.astype(F16))
    halves = split_by_core(grads, outer, width)
    pair = lax.all_to_all(halves, "core", 0, 0, tiled=True).astype(F32)
    partial = ((pair[0] + pair[1]) * PAIR_SCALE).astype(F16)
    parts = lax.all_to_all(partial, "outer", 0, 0, tiled=True)
    sums = jnp.sum(parts.astype(F32), axis=0) * (1.0 / PAIR_SCALE)
    outgoing = pl.pallas_call(
        rows_kernel,
        in_specs=[SMEM] * 2 + [VMEM] * 4,
        out_specs=VMEM,
        out_shape=jax.ShapeDtypeStruct((devices, 4 * tiles + 2 * ROW, LANES), F32),
        scratch_shapes=[pltpu.VMEM((homes + 1, 4 * tiles, LANES), F32)],
        compiler_params=pltpu.CompilerParams(vmem_limit_bytes=16 * 2**20),
        cost_estimate=cost(1 << 18),
    )(slot, asked, sums, weights, first, second)
    arrived = lax.all_to_all(outgoing.astype(F16), "expert", 0, 0, tiled=True)
    extras = arrived[:, 4 * tiles : 4 * tiles + ROW, :].astype(F32)
    state = lax.dynamic_index_in_dim(held, place(source), 0, keepdims=False)[: 3 * tiles]
    moved = lax.dynamic_slice(arrived, (source, 4 * tiles + ROW, 0), (1, tiles, LANES))
    copied = lax.dynamic_slice(arrived, (extra_source, 0, 0), (1, 4 * tiles, LANES))
    got = jnp.concatenate([state, moved[0], copied[0]], axis=0).astype(F32)
    return pl.pallas_call(
        final_kernel,
        in_specs=[SMEM] * 3 + [VMEM] * 6,
        out_specs=[VMEM] * 3,
        out_shape=[
            jax.ShapeDtypeStruct((homes + 1, width), BF16),
            jax.ShapeDtypeStruct((homes, width), F32),
            jax.ShapeDtypeStruct((homes, width), F32),
        ],
        scratch_shapes=[pltpu.VMEM((homes + 1, ROW, LANES), F32), pltpu.VMEM((3 * homes, width), F32)],
        compiler_params=pltpu.CompilerParams(vmem_limit_bytes=16 * 2**20),
        cost_estimate=cost(1 << 18),
    )(slot, adds, extra_adds, sums, extras, got, weights, first, second)


def solution(mesh):
    groups, devices = mesh.devices.shape
    grid = Mesh(mesh.devices.reshape(groups // 2, 2, devices), ("outer", "core", "expert"))
    dp = ("outer", "core")
    placed = (P(dp, "expert", None), P("expert", dp), P("expert", dp), P("expert", dp), P(), P(), P(), P())
    return jax.shard_map(
        per_device,
        mesh=grid,
        in_specs=placed,
        out_specs=(P("expert", dp), P("expert", dp), P("expert", dp)),
        check_vma=False,
    )
```

```python
import jax
import jax.numpy as jnp
from jax import lax
from jax.experimental import pallas as pl
from jax.experimental.pallas import tpu as pltpu
from jax.sharding import Mesh
from jax.sharding import PartitionSpec as P

bias_first = 0.9999734386011124
bias_second = 0.994079470779696
LANES = 128
PLANE = 4
ORDER = (0, 2, 1, 3)
ROW = 16
PAIR_SCALE = 4096.0
SUM_SCALE = 256.0
STATE_SCALE = 16384.0

F32 = jnp.float32
F16 = jnp.float16
BF16 = jnp.bfloat16
VMEM = pl.BlockSpec(memory_space=pltpu.VMEM)
SMEM = pl.BlockSpec(memory_space=pltpu.SMEM)


def cost(n):
    return pl.CostEstimate(flops=n, bytes_accessed=4 * n, transcendentals=0)


def split_kernel(homes, width, steps, grads_ref, out_ref, line):
    tiles = width // LANES
    line[...] = jnp.zeros_like(line)
    for j in range(steps):
        for c in range(2):
            at = (2 * j + c) * width
            block = grads_ref[0, :, at : at + width].astype(F32)
            for t in range(0, tiles, 2):
                low = block[:homes, t * LANES : (t + 1) * LANES]
                high = block[:homes, (t + 1) * LANES : (t + 2) * LANES]
                out_ref[c, j, t * homes : (t + 2) * homes, :] = jnp.concatenate([low, high], axis=0).astype(BF16)
            for t in range(tiles):
                line[t : t + 1, :] = block[homes : homes + 1, t * LANES : (t + 1) * LANES]
            out_ref[c, j, tiles * homes : tiles * homes + ROW, :] = line[...].astype(BF16)


def split_by_core(grads, outer, width):
    homes = grads.shape[1] - 1
    rows = (width // LANES) * homes + ROW
    steps = 4 if outer % 4 == 0 else 1
    return pl.pallas_call(
        lambda *refs: split_kernel(homes, width, steps, *refs),
        grid=(outer // steps,),
        in_specs=[pl.BlockSpec((1, homes + 1, steps * 2 * width), lambda i: (0, 0, i))],
        out_specs=pl.BlockSpec((2, steps, rows, LANES), lambda i: (0, i, 0, 0)),
        out_shape=jax.ShapeDtypeStruct((2, outer, rows, LANES), BF16),
        scratch_shapes=[pltpu.VMEM((ROW, LANES), F32)],
        compiler_params=pltpu.CompilerParams(vmem_limit_bytes=16 * 2**20),
        cost_estimate=cost(1 << 19),
    )(grads)


def starts(tiles):
    per = -(-tiles // PLANE)
    return per, [min(y * per, tiles - per) for y in range(PLANE)]


def rows_kernel(slot_ref, mine_ref, asked_ref, moves_ref, wants_ref, sums_ref, held_ref, out_ref, state_a, state_b, sent):
    homes = sent.shape[0]
    tiles = held_ref.shape[3] // LANES
    per, _ = starts(tiles)
    mine = mine_ref[0]
    first_tile = jnp.minimum(mine * per, tiles - per)
    state_a[...] = jnp.zeros_like(state_a)
    state_b[...] = jnp.zeros_like(state_b)
    for r in range(PLANE):
        base = jnp.bitwise_xor(mine, ORDER[r]) * homes
        for n in range(3):
            for k in range(per):
                at = pl.multiple_of((first_tile + k) * LANES, LANES)
                value = held_ref[r, n, :, pl.ds(at, LANES)]
                for i in range(homes):
                    state_a[base + i, n * per + k : n * per + k + 1, :] = value[i : i + 1, :]
                    state_b[base + i, (3 + n) * per + k : (3 + n) * per + k + 1, :] = value[i : i + 1, :]
    sums = sums_ref[...] * SUM_SCALE
    slot = slot_ref[0]
    sent[...] = jnp.zeros_like(sent)
    for i in range(homes):
        for t in range(tiles):
            sent[i, tiles + t : tiles + t + 1, :] = sums[t * homes + i : t * homes + i + 1, :]
    leaving = sent[slot]
    for t in range(tiles):
        at = tiles * homes + t
        for i in range(homes):
            row = 2 * tiles + t
            sent[i, row : row + 1, :] = sent[i, tiles + t : tiles + t + 1, :]
            sent[i, tiles + t : tiles + t + 1, :] = leaving[tiles + t : tiles + t + 1, :]
            sent[i, t : t + 1, :] = sums[at : at + 1, :]
    head = 6 * per
    for d in range(out_ref.shape[0]):
        out_ref[d, :head, :] = state_a[moves_ref[d]] + state_b[wants_ref[d]]
        out_ref[d, head:, :] = sent[asked_ref[d]]


def adam(total, base, first, second):
    moment1 = 0.9 * first + 0.1 * total
    moment2 = 0.95 * second + 0.05 * total * total
    step = moment1 / bias_first / (jnp.sqrt(moment2 / bias_second) + 1e-08)
    return base - 0.02 * (step + 0.1 * base), moment1, moment2


def final_kernel(
    slot_ref, adds_ref, extra_adds_ref, sums_ref, extras_ref, states_ref, totals_ref, w_ref, f_ref, s_ref, nw_ref, nf_ref, ns_ref, acc, flat
):
    homes, width = f_ref.shape
    tiles = width // LANES
    per, firsts = starts(tiles)
    slot = slot_ref[0]
    acc[...] = jnp.zeros_like(acc)
    for s in range(extras_ref.shape[0]):
        to = adds_ref[s]

        @pl.when(to >= 0)
        def _():
            acc[to] += extras_ref[s]

        @pl.when(extra_adds_ref[s] > 0)
        def _():
            acc[homes] += extras_ref[s]

    for y in range(PLANE):
        for k in range(per):
            cols = slice((firsts[y] + k) * LANES, (firsts[y] + k + 1) * LANES)
            for h in range(2):
                for n in range(3):
                    to = 2 * homes + 4 * h + n
                    at = (3 * h + n) * per + k
                    flat[to : to + 1, cols] = states_ref[h, y, at : at + 1, :]
    for t in range(tiles):
        cols = slice(t * LANES, (t + 1) * LANES)
        for i in range(homes + 1):
            flat[i : i + 1, cols] = acc[i, t : t + 1, :]
        for h in range(2):
            to = 2 * homes + 4 * h + 3
            at = (h + 1) * tiles + t
            flat[to : to + 1, cols] = totals_ref[h, at : at + 1, :]
    is_new = lax.broadcasted_iota(jnp.int32, (homes, LANES), 0) == slot
    for t in range(tiles):
        cols = slice(t * LANES, (t + 1) * LANES)
        got = flat[2 * homes : 2 * homes + 8, cols]
        own = sums_ref[t * homes : (t + 1) * homes, :]
        total = (flat[:homes, cols] + jnp.where(is_new, got[3:4], own * SUM_SCALE)) * (1.0 / SUM_SCALE)
        base = jnp.where(is_new, got[0:1] * (1.0 / STATE_SCALE), w_ref[:, cols].astype(F32))
        first = jnp.where(is_new, got[1:2] * (1.0 / STATE_SCALE), f_ref[:, cols])
        second = jnp.where(is_new, got[2:3] * (1.0 / STATE_SCALE), s_ref[:, cols])
        updated, moment1, moment2 = adam(total, base, first, second)
        total = (flat[homes : homes + 1, cols] + got[7:8]) * (1.0 / SUM_SCALE)
        state = got * (1.0 / STATE_SCALE)
        extra, _, _ = adam(total, state[4:5], state[5:6], state[6:7])
        nf_ref[:, cols] = moment1
        ns_ref[:, cols] = moment2
        nw_ref[:, cols] = jnp.concatenate([updated, extra], axis=0).astype(BF16)


def routes(homes, old_home, old_extra, new_home, new_extra):
    me = lax.axis_index("expert")
    my_new = lax.dynamic_slice_in_dim(new_home, me * homes, homes)
    my_old = lax.dynamic_slice_in_dim(old_home, me * homes, homes)
    wanted = lax.dynamic_slice_in_dim(new_extra, me, 1)
    ids = jnp.arange(homes, dtype=jnp.int32)
    slot = jnp.sum(jnp.where(my_old != my_new, ids, 0)).reshape(1)
    places = jnp.arange(old_home.shape[0], dtype=jnp.int32)
    device = jnp.arange(new_extra.shape[0], dtype=jnp.int32)
    arrives = (old_home != new_home)[None, :] & (places[None, :] // homes == device[:, None])
    arriving = jnp.sum(jnp.where(arrives, new_home[None, :], 0), axis=1)
    moves = jnp.sum(jnp.where(arriving[:, None] == old_home[None, :], places[None, :], 0), axis=1)
    wants = jnp.sum(jnp.where(new_extra[:, None] == old_home[None, :], places[None, :], 0), axis=1)
    source = jnp.sum(jnp.where(device == me, moves // homes, 0))
    extra_source = jnp.sum(jnp.where(device == me, wants // homes, 0))
    asked = jnp.where(wants // homes == me, wants % homes, 0)
    adds = jnp.sum(jnp.where(old_extra[:, None] == my_new[None, :], ids[None, :] + 1, 0), axis=1) - 1
    extra_adds = (old_extra == wanted).astype(jnp.int32)
    plane = PLANE * homes
    return slot, source, extra_source, asked, moves % plane, wants % plane, adds, extra_adds


def share_states(weights, first, second):
    devices = lax.axis_size("expert")
    states = jnp.stack([weights.astype(F32), first, second])
    held = (states * STATE_SCALE).astype(F16)[None]
    for bit in (2, 1):
        other = lax.ppermute(held, "expert", [(i, i ^ bit) for i in range(devices)])
        held = jnp.concatenate([held, other], axis=0)
    return held.astype(F32)


def per_device(grads, weights, first, second, old_home, old_extra, new_home, new_extra):
    homes, width = weights.shape
    tiles = width // LANES
    outer = lax.axis_size("outer")
    devices = lax.axis_size("expert")
    tables = routes(homes, old_home, old_extra, new_home, new_extra)
    slot, source, extra_source, asked, moves, wants, adds, extra_adds = tables
    held = share_states(weights, first, second)
    mine = (lax.axis_index("expert") % PLANE).astype(jnp.int32).reshape(1)
    halves = split_by_core(grads, outer, width)
    pair = lax.all_to_all(halves, "core", 0, 0, tiled=True).astype(F32)
    partial = ((pair[0] + pair[1]) * PAIR_SCALE).astype(F16)
    parts = lax.all_to_all(partial, "outer", 0, 0, tiled=True)
    sums = jnp.sum(parts.astype(F32), axis=0) * (1.0 / PAIR_SCALE)
    per, _ = starts(tiles)
    head = 6 * per
    tail = -(-3 * tiles // 8) * 8
    outgoing = pl.pallas_call(
        rows_kernel,
        in_specs=[SMEM] * 5 + [VMEM] * 2,
        out_specs=VMEM,
        out_shape=jax.ShapeDtypeStruct((devices, head + tail, LANES), F32),
        scratch_shapes=[
            pltpu.VMEM((PLANE * homes, head, LANES), F32),
            pltpu.VMEM((PLANE * homes, head, LANES), F32),
            pltpu.VMEM((homes, tail, LANES), F32),
        ],
        compiler_params=pltpu.CompilerParams(vmem_limit_bytes=16 * 2**20),
        cost_estimate=cost(1 << 18),
    )(slot, mine, asked, moves, wants, sums, held)
    arrived = lax.all_to_all(outgoing.astype(F16), "expert", 0, 0, tiled=True)
    extras = arrived[:, head : head + ROW, :].astype(F32)
    both = (source, extra_source)
    states = jnp.stack([lax.dynamic_slice(arrived, (at // PLANE * PLANE, 0, 0), (PLANE, head, LANES)) for at in both])
    totals = jnp.concatenate([lax.dynamic_slice(arrived, (at, head, 0), (1, tail, LANES)) for at in both])
    states = states.astype(F32)
    totals = totals.astype(F32)
    return pl.pallas_call(
        final_kernel,
        in_specs=[SMEM] * 3 + [VMEM] * 7,
        out_specs=[VMEM] * 3,
        out_shape=[
            jax.ShapeDtypeStruct((homes + 1, width), BF16),
            jax.ShapeDtypeStruct((homes, width), F32),
            jax.ShapeDtypeStruct((homes, width), F32),
        ],
        scratch_shapes=[pltpu.VMEM((homes + 1, ROW, LANES), F32), pltpu.VMEM((3 * homes, width), F32)],
        compiler_params=pltpu.CompilerParams(vmem_limit_bytes=16 * 2**20),
        cost_estimate=cost(1 << 18),
    )(slot, adds, extra_adds, sums, extras, states, totals, weights, first, second)


def solution(mesh):
    groups, devices = mesh.devices.shape
    grid = Mesh(mesh.devices.reshape(groups // 2, 2, devices), ("outer", "core", "expert"))
    dp = ("outer", "core")
    placed = (P(dp, "expert", None), P("expert", dp), P("expert", dp), P("expert", dp), P(), P(), P(), P())
    return jax.shard_map(
        per_device,
        mesh=grid,
        in_specs=placed,
        out_specs=(P("expert", dp), P("expert", dp), P("expert", dp)),
        check_vma=False,
    )
```

```python
import jax
import jax.numpy as jnp
from jax import lax
from jax.experimental import pallas as pl
from jax.experimental.pallas import tpu as pltpu
from jax.sharding import Mesh
from jax.sharding import PartitionSpec as P

bias_first = 0.9999734386011124
bias_second = 0.994079470779696
LANES = 128
PLANE = 4
ORDER = (0, 2, 1, 3)
ROW = 16
PAIR_SCALE = 4096.0
SUM_SCALE = 256.0
STATE_SCALE = 16384.0

F32 = jnp.float32
F16 = jnp.float16
BF16 = jnp.bfloat16
VMEM = pl.BlockSpec(memory_space=pltpu.VMEM)
SMEM = pl.BlockSpec(memory_space=pltpu.SMEM)


def cost(n):
    return pl.CostEstimate(flops=n, bytes_accessed=4 * n, transcendentals=0)


def split_kernel(homes, width, steps, grads_ref, out_ref, line):
    tiles = width // LANES
    line[...] = jnp.zeros_like(line)
    for j in range(steps):
        for c in range(2):
            at = (2 * j + c) * width
            block = grads_ref[0, :, at : at + width].astype(F32)
            for t in range(0, tiles, 2):
                low = block[:homes, t * LANES : (t + 1) * LANES]
                high = block[:homes, (t + 1) * LANES : (t + 2) * LANES]
                out_ref[c, j, t * homes : (t + 2) * homes, :] = jnp.concatenate([low, high], axis=0).astype(BF16)
            for t in range(tiles):
                line[t : t + 1, :] = block[homes : homes + 1, t * LANES : (t + 1) * LANES]
            out_ref[c, j, tiles * homes : tiles * homes + ROW, :] = line[...].astype(BF16)


def split_by_core(grads, outer, width):
    homes = grads.shape[1] - 1
    rows = (width // LANES) * homes + ROW
    steps = 4 if outer % 4 == 0 else 1
    return pl.pallas_call(
        lambda *refs: split_kernel(homes, width, steps, *refs),
        grid=(outer // steps,),
        in_specs=[pl.BlockSpec((1, homes + 1, steps * 2 * width), lambda i: (0, 0, i))],
        out_specs=pl.BlockSpec((2, steps, rows, LANES), lambda i: (0, i, 0, 0)),
        out_shape=jax.ShapeDtypeStruct((2, outer, rows, LANES), BF16),
        scratch_shapes=[pltpu.VMEM((ROW, LANES), F32)],
        compiler_params=pltpu.CompilerParams(vmem_limit_bytes=16 * 2**20),
        cost_estimate=cost(1 << 19),
    )(grads)


def starts(tiles):
    per = -(-tiles // PLANE)
    return per, [min(y * per, tiles - per) for y in range(PLANE)]


def rows_kernel(slot_ref, mine_ref, asked_ref, moves_ref, wants_ref, sums_ref, held_ref, out_ref, state_a, state_b, sent):
    homes = sent.shape[0]
    tiles = held_ref.shape[3] // LANES
    per, _ = starts(tiles)
    mine = mine_ref[0]
    first_tile = jnp.minimum(mine * per, tiles - per)
    state_a[...] = jnp.zeros_like(state_a)
    state_b[...] = jnp.zeros_like(state_b)
    for r in range(PLANE):
        base = jnp.bitwise_xor(mine, ORDER[r]) * homes
        for n in range(3):
            for k in range(per):
                at = pl.multiple_of((first_tile + k) * LANES, LANES)
                value = held_ref[r, n, :, pl.ds(at, LANES)]
                for i in range(homes):
                    state_a[base + i, n * per + k : n * per + k + 1, :] = value[i : i + 1, :]
                    state_b[base + i, (3 + n) * per + k : (3 + n) * per + k + 1, :] = value[i : i + 1, :]
    sums = sums_ref[...] * SUM_SCALE
    slot = slot_ref[0]
    sent[...] = jnp.zeros_like(sent)
    for i in range(homes):
        for t in range(tiles):
            sent[i, tiles + t : tiles + t + 1, :] = sums[t * homes + i : t * homes + i + 1, :]
    leaving = sent[slot]
    for t in range(tiles):
        at = tiles * homes + t
        for i in range(homes):
            row = 2 * tiles + t
            sent[i, row : row + 1, :] = sent[i, tiles + t : tiles + t + 1, :]
            sent[i, tiles + t : tiles + t + 1, :] = leaving[tiles + t : tiles + t + 1, :]
            sent[i, t : t + 1, :] = sums[at : at + 1, :]
    head = 6 * per
    for d in range(out_ref.shape[0]):
        out_ref[d, :head, :] = state_a[moves_ref[d]] + state_b[wants_ref[d]]
        out_ref[d, head:, :] = sent[asked_ref[d]]


def adam(total, base, first, second):
    moment1 = 0.9 * first + 0.1 * total
    moment2 = 0.95 * second + 0.05 * total * total
    step = moment1 / bias_first / (jnp.sqrt(moment2 / bias_second) + 1e-08)
    return base - 0.02 * (step + 0.1 * base), moment1, moment2


def final_kernel(
    slot_ref, adds_ref, extra_adds_ref, sums_ref, extras_ref, states_ref, totals_ref, w_ref, f_ref, s_ref, nw_ref, nf_ref, ns_ref, acc, flat
):
    homes, width = f_ref.shape
    tiles = width // LANES
    per, firsts = starts(tiles)
    slot = slot_ref[0]
    acc[...] = jnp.zeros_like(acc)
    for s in range(extras_ref.shape[0]):
        to = adds_ref[s]

        @pl.when(to >= 0)
        def _():
            acc[to] += extras_ref[s]

        @pl.when(extra_adds_ref[s] > 0)
        def _():
            acc[homes] += extras_ref[s]

    for y in range(PLANE):
        for k in range(per):
            cols = slice((firsts[y] + k) * LANES, (firsts[y] + k + 1) * LANES)
            for h in range(2):
                for n in range(3):
                    to = 2 * homes + 4 * h + n
                    at = (3 * h + n) * per + k
                    flat[to : to + 1, cols] = states_ref[h, y, at : at + 1, :]
    for t in range(tiles):
        cols = slice(t * LANES, (t + 1) * LANES)
        for i in range(homes + 1):
            flat[i : i + 1, cols] = acc[i, t : t + 1, :]
        for h in range(2):
            to = 2 * homes + 4 * h + 3
            at = (h + 1) * tiles + t
            flat[to : to + 1, cols] = totals_ref[h, at : at + 1, :]
    is_new = lax.broadcasted_iota(jnp.int32, (homes, LANES), 0) == slot
    for t in range(tiles):
        cols = slice(t * LANES, (t + 1) * LANES)
        got = flat[2 * homes : 2 * homes + 8, cols]
        own = sums_ref[t * homes : (t + 1) * homes, :]
        total = (flat[:homes, cols] + jnp.where(is_new, got[3:4], own * SUM_SCALE)) * (1.0 / SUM_SCALE)
        base = jnp.where(is_new, got[0:1] * (1.0 / STATE_SCALE), w_ref[:, cols].astype(F32))
        first = jnp.where(is_new, got[1:2] * (1.0 / STATE_SCALE), f_ref[:, cols])
        second = jnp.where(is_new, got[2:3] * (1.0 / STATE_SCALE), s_ref[:, cols])
        updated, moment1, moment2 = adam(total, base, first, second)
        total = (flat[homes : homes + 1, cols] + got[7:8]) * (1.0 / SUM_SCALE)
        state = got * (1.0 / STATE_SCALE)
        extra, _, _ = adam(total, state[4:5], state[5:6], state[6:7])
        nf_ref[:, cols] = moment1
        ns_ref[:, cols] = moment2
        nw_ref[:, cols] = jnp.concatenate([updated, extra], axis=0).astype(BF16)


def plane_stride():
    return max(lax.axis_size("expert") // 8, 1)


def routes(homes, old_home, old_extra, new_home, new_extra):
    me = lax.axis_index("expert")
    my_new = lax.dynamic_slice_in_dim(new_home, me * homes, homes)
    my_old = lax.dynamic_slice_in_dim(old_home, me * homes, homes)
    wanted = lax.dynamic_slice_in_dim(new_extra, me, 1)
    ids = jnp.arange(homes, dtype=jnp.int32)
    slot = jnp.sum(jnp.where(my_old != my_new, ids, 0)).reshape(1)
    places = jnp.arange(old_home.shape[0], dtype=jnp.int32)
    device = jnp.arange(new_extra.shape[0], dtype=jnp.int32)
    arrives = (old_home != new_home)[None, :] & (places[None, :] // homes == device[:, None])
    arriving = jnp.sum(jnp.where(arrives, new_home[None, :], 0), axis=1)
    moves = jnp.sum(jnp.where(arriving[:, None] == old_home[None, :], places[None, :], 0), axis=1)
    wants = jnp.sum(jnp.where(new_extra[:, None] == old_home[None, :], places[None, :], 0), axis=1)
    source = jnp.sum(jnp.where(device == me, moves // homes, 0))
    extra_source = jnp.sum(jnp.where(device == me, wants // homes, 0))
    asked = jnp.where(wants // homes == me, wants % homes, 0)
    adds = jnp.sum(jnp.where(old_extra[:, None] == my_new[None, :], ids[None, :] + 1, 0), axis=1) - 1
    extra_adds = (old_extra == wanted).astype(jnp.int32)
    stride = plane_stride()

    def in_plane(place):
        return (place // homes // stride) % PLANE * homes + place % homes

    return slot, source, extra_source, asked, in_plane(moves), in_plane(wants), adds, extra_adds


def share_states(weights, first, second):
    devices = lax.axis_size("expert")
    states = jnp.stack([weights.astype(F32), first, second])
    held = (states * STATE_SCALE).astype(F16)[None]
    for step in (2, 1):
        bit = step * plane_stride()
        other = lax.ppermute(held, "expert", [(i, i ^ bit) for i in range(devices)])
        held = jnp.concatenate([held, other], axis=0)
    return held.astype(F32)


def per_device(grads, weights, first, second, old_home, old_extra, new_home, new_extra):
    homes, width = weights.shape
    tiles = width // LANES
    outer = lax.axis_size("outer")
    devices = lax.axis_size("expert")
    tables = routes(homes, old_home, old_extra, new_home, new_extra)
    slot, source, extra_source, asked, moves, wants, adds, extra_adds = tables
    held = share_states(weights, first, second)
    mine = (lax.axis_index("expert") // plane_stride() % PLANE).astype(jnp.int32).reshape(1)
    halves = split_by_core(grads, outer, width)
    pair = lax.all_to_all(halves, "core", 0, 0, tiled=True).astype(F32)
    partial = ((pair[0] + pair[1]) * PAIR_SCALE).astype(F16)
    parts = lax.all_to_all(partial, "outer", 0, 0, tiled=True)
    sums = jnp.sum(parts.astype(F32), axis=0) * (1.0 / PAIR_SCALE)
    per, _ = starts(tiles)
    head = 6 * per
    tail = -(-3 * tiles // 8) * 8
    outgoing = pl.pallas_call(
        rows_kernel,
        in_specs=[SMEM] * 5 + [VMEM] * 2,
        out_specs=VMEM,
        out_shape=jax.ShapeDtypeStruct((devices, head + tail, LANES), F32),
        scratch_shapes=[
            pltpu.VMEM((PLANE * homes, head, LANES), F32),
            pltpu.VMEM((PLANE * homes, head, LANES), F32),
            pltpu.VMEM((homes, tail, LANES), F32),
        ],
        compiler_params=pltpu.CompilerParams(vmem_limit_bytes=16 * 2**20),
        cost_estimate=cost(1 << 18),
    )(slot, mine, asked, moves, wants, sums, held)
    arrived = lax.all_to_all(outgoing.astype(F16), "expert", 0, 0, tiled=True)
    extras = arrived[:, head : head + ROW, :].astype(F32)
    both = (source, extra_source)
    stride = plane_stride()
    planes = arrived.reshape(devices // (PLANE * stride), PLANE, stride, head + tail, LANES)
    size = (1, PLANE, 1, head, LANES)
    states = [lax.dynamic_slice(planes, (at // (PLANE * stride), 0, at % stride, 0, 0), size) for at in both]
    states = jnp.stack(states).reshape(2, PLANE, head, LANES)
    totals = jnp.concatenate([lax.dynamic_slice(arrived, (at, head, 0), (1, tail, LANES)) for at in both])
    states = states.astype(F32)
    totals = totals.astype(F32)
    return pl.pallas_call(
        final_kernel,
        in_specs=[SMEM] * 3 + [VMEM] * 7,
        out_specs=[VMEM] * 3,
        out_shape=[
            jax.ShapeDtypeStruct((homes + 1, width), BF16),
            jax.ShapeDtypeStruct((homes, width), F32),
            jax.ShapeDtypeStruct((homes, width), F32),
        ],
        scratch_shapes=[pltpu.VMEM((homes + 1, ROW, LANES), F32), pltpu.VMEM((3 * homes, width), F32)],
        compiler_params=pltpu.CompilerParams(vmem_limit_bytes=16 * 2**20),
        cost_estimate=cost(1 << 18),
    )(slot, adds, extra_adds, sums, extras, states, totals, weights, first, second)


def solution(mesh):
    groups, devices = mesh.devices.shape
    grid = Mesh(mesh.devices.reshape(groups // 2, 2, devices), ("outer", "core", "expert"))
    dp = ("outer", "core")
    placed = (P(dp, "expert", None), P("expert", dp), P("expert", dp), P("expert", dp), P(), P(), P(), P())
    return jax.shard_map(
        per_device,
        mesh=grid,
        in_specs=placed,
        out_specs=(P("expert", dp), P("expert", dp), P("expert", dp)),
        check_vma=False,
    )
```

```python
import jax
import jax.numpy as jnp
from jax import lax
from jax.experimental import pallas as pl
from jax.experimental.pallas import tpu as pltpu
from jax.sharding import Mesh
from jax.sharding import PartitionSpec as P

bias_first = 0.9999734386011124
bias_second = 0.994079470779696
LANES = 128
PLANE = 4
ORDER = (0, 2, 1, 3)
ROW = 16
PAIR_SCALE = 4096.0
SUM_SCALE = 256.0
STATE_SCALE = 16384.0

F32 = jnp.float32
F16 = jnp.float16
BF16 = jnp.bfloat16
VMEM = pl.BlockSpec(memory_space=pltpu.VMEM)
SMEM = pl.BlockSpec(memory_space=pltpu.SMEM)


def cost(n):
    return pl.CostEstimate(flops=n, bytes_accessed=4 * n, transcendentals=0)


def split_kernel(homes, width, steps, grads_ref, out_ref, line):
    tiles = width // LANES
    line[...] = jnp.zeros_like(line)
    for j in range(steps):
        for c in range(2):
            at = (2 * j + c) * width
            block = grads_ref[0, :, at : at + width].astype(F32)
            for t in range(0, tiles, 2):
                low = block[:homes, t * LANES : (t + 1) * LANES]
                high = block[:homes, (t + 1) * LANES : (t + 2) * LANES]
                out_ref[c, j, t * homes : (t + 2) * homes, :] = jnp.concatenate([low, high], axis=0).astype(BF16)
            for t in range(tiles):
                line[t : t + 1, :] = block[homes : homes + 1, t * LANES : (t + 1) * LANES]
            out_ref[c, j, tiles * homes : tiles * homes + ROW, :] = line[...].astype(BF16)


def split_by_core(grads, outer, width):
    homes = grads.shape[1] - 1
    rows = (width // LANES) * homes + ROW
    steps = 4 if outer % 4 == 0 else 1
    return pl.pallas_call(
        lambda *refs: split_kernel(homes, width, steps, *refs),
        grid=(outer // steps,),
        in_specs=[pl.BlockSpec((1, homes + 1, steps * 2 * width), lambda i: (0, 0, i))],
        out_specs=pl.BlockSpec((2, steps, rows, LANES), lambda i: (0, i, 0, 0)),
        out_shape=jax.ShapeDtypeStruct((2, outer, rows, LANES), BF16),
        scratch_shapes=[pltpu.VMEM((ROW, LANES), F32)],
        compiler_params=pltpu.CompilerParams(vmem_limit_bytes=16 * 2**20),
        cost_estimate=cost(1 << 19),
    )(grads)


def starts(tiles):
    per = -(-tiles // PLANE)
    return per, [min(y * per, tiles - per) for y in range(PLANE)]


def states_kernel(mine_ref, moves_ref, wants_ref, held_ref, out_ref, state_a, state_b):
    homes, width = held_ref.shape[2:]
    tiles = width // LANES
    per, _ = starts(tiles)
    mine = mine_ref[0]
    first_tile = jnp.minimum(mine * per, tiles - per)
    state_a[...] = jnp.zeros_like(state_a)
    state_b[...] = jnp.zeros_like(state_b)
    for r in range(PLANE):
        base = jnp.bitwise_xor(mine, ORDER[r]) * homes
        for n in range(3):
            for k in range(per):
                at = pl.multiple_of((first_tile + k) * LANES, LANES)
                value = held_ref[r, n, :, pl.ds(at, LANES)]
                for i in range(homes):
                    state_a[base + i, n * per + k : n * per + k + 1, :] = value[i : i + 1, :]
                    state_b[base + i, (3 + n) * per + k : (3 + n) * per + k + 1, :] = value[i : i + 1, :]
    for d in range(out_ref.shape[0]):
        out_ref[d] = state_a[moves_ref[d]] + state_b[wants_ref[d]]


def sums_kernel(slot_ref, asked_ref, sums_ref, heads_ref, out_ref, home, fixed):
    homes = home.shape[0]
    tiles = (sums_ref.shape[0] - ROW) // homes
    home[...] = jnp.zeros_like(home)
    fixed[...] = jnp.zeros_like(fixed)
    slot = slot_ref[0]
    for t in range(tiles):
        tile = sums_ref[t * homes : (t + 1) * homes, :] * SUM_SCALE
        row = 2 * tiles + t
        for i in range(homes):
            home[i, row : row + 1, :] = tile[i : i + 1, :]
        at = tiles * homes + t
        fixed[t : t + 1, :] = sums_ref[at : at + 1, :] * SUM_SCALE
    for t in range(tiles):
        row = 2 * tiles + t
        fixed[tiles + t : tiles + t + 1, :] = home[slot, row : row + 1, :]
    keep = fixed[...]
    head = heads_ref.shape[1]
    for d in range(out_ref.shape[0]):
        out_ref[d, :head, :] = heads_ref[d]
        out_ref[d, head:, :] = keep + home[asked_ref[d]]


def adam(total, base, first, second):
    moment1 = 0.9 * first + 0.1 * total
    moment2 = 0.95 * second + 0.05 * total * total
    step = moment1 / bias_first / (jnp.sqrt(moment2 / bias_second) + 1e-08)
    return base - 0.02 * (step + 0.1 * base), moment1, moment2


def final_kernel(
    slot_ref, adds_ref, extra_adds_ref, sums_ref, extras_ref, states_ref, totals_ref, w_ref, f_ref, s_ref, nw_ref, nf_ref, ns_ref, acc, flat
):
    homes, width = f_ref.shape
    tiles = width // LANES
    per, firsts = starts(tiles)
    slot = slot_ref[0]
    acc[...] = jnp.zeros_like(acc)
    copied = jnp.zeros(acc.shape[1:], F32)
    for s in range(extras_ref.shape[0]):
        acc[adds_ref[s]] += extras_ref[s]
        copied += extras_ref[s] * extra_adds_ref[s].astype(F32)
    acc[homes] = copied
    for y in range(PLANE):
        for k in range(per):
            cols = slice((firsts[y] + k) * LANES, (firsts[y] + k + 1) * LANES)
            for h in range(2):
                for n in range(3):
                    to = 2 * homes + 4 * h + n
                    at = (3 * h + n) * per + k
                    flat[to : to + 1, cols] = states_ref[h, y, at : at + 1, :]
    for t in range(tiles):
        cols = slice(t * LANES, (t + 1) * LANES)
        for i in range(homes + 1):
            flat[i : i + 1, cols] = acc[i, t : t + 1, :]
        for h in range(2):
            to = 2 * homes + 4 * h + 3
            at = (h + 1) * tiles + t
            flat[to : to + 1, cols] = totals_ref[h, at : at + 1, :]
    is_new = lax.broadcasted_iota(jnp.int32, (homes, LANES), 0) == slot
    for t in range(tiles):
        cols = slice(t * LANES, (t + 1) * LANES)
        got = flat[2 * homes : 2 * homes + 8, cols]
        own = sums_ref[t * homes : (t + 1) * homes, :]
        total = (flat[:homes, cols] + jnp.where(is_new, got[3:4], own * SUM_SCALE)) * (1.0 / SUM_SCALE)
        base = jnp.where(is_new, got[0:1] * (1.0 / STATE_SCALE), w_ref[:, cols].astype(F32))
        first = jnp.where(is_new, got[1:2] * (1.0 / STATE_SCALE), f_ref[:, cols])
        second = jnp.where(is_new, got[2:3] * (1.0 / STATE_SCALE), s_ref[:, cols])
        updated, moment1, moment2 = adam(total, base, first, second)
        total = (flat[homes : homes + 1, cols] + got[7:8]) * (1.0 / SUM_SCALE)
        state = got * (1.0 / STATE_SCALE)
        extra, _, _ = adam(total, state[4:5], state[5:6], state[6:7])
        nf_ref[:, cols] = moment1
        ns_ref[:, cols] = moment2
        nw_ref[:, cols] = jnp.concatenate([updated, extra], axis=0).astype(BF16)


def plane_stride():
    return max(lax.axis_size("expert") // 8, 1)


def routes(homes, old_home, old_extra, new_home, new_extra):
    me = lax.axis_index("expert")
    my_new = lax.dynamic_slice_in_dim(new_home, me * homes, homes)
    my_old = lax.dynamic_slice_in_dim(old_home, me * homes, homes)
    wanted = lax.dynamic_slice_in_dim(new_extra, me, 1)
    ids = jnp.arange(homes, dtype=jnp.int32)
    slot = jnp.sum(jnp.where(my_old != my_new, ids, 0)).reshape(1)
    places = jnp.arange(old_home.shape[0], dtype=jnp.int32)
    device = jnp.arange(new_extra.shape[0], dtype=jnp.int32)
    arrives = (old_home != new_home)[None, :] & (places[None, :] // homes == device[:, None])
    arriving = jnp.sum(jnp.where(arrives, new_home[None, :], 0), axis=1)
    moves = jnp.sum(jnp.where(arriving[:, None] == old_home[None, :], places[None, :], 0), axis=1)
    wants = jnp.sum(jnp.where(new_extra[:, None] == old_home[None, :], places[None, :], 0), axis=1)
    source = jnp.sum(jnp.where(device == me, moves // homes, 0))
    extra_source = jnp.sum(jnp.where(device == me, wants // homes, 0))
    asked = jnp.where(wants // homes == me, wants % homes, 0)
    spare = homes + 1
    adds = jnp.sum(jnp.where(old_extra[:, None] == my_new[None, :], ids[None, :] - spare, 0), axis=1) + spare
    extra_adds = (old_extra == wanted).astype(jnp.int32)
    stride = plane_stride()

    def in_plane(place):
        return (place // homes // stride) % PLANE * homes + place % homes

    return slot, source, extra_source, asked, in_plane(moves), in_plane(wants), adds, extra_adds


def share_states(weights, first, second):
    devices = lax.axis_size("expert")
    states = jnp.stack([weights.astype(F32), first, second])
    held = (states * STATE_SCALE).astype(F16)[None]
    for step in (2, 1):
        bit = step * plane_stride()
        other = lax.ppermute(held, "expert", [(i, i ^ bit) for i in range(devices)])
        held = jnp.concatenate([held, other], axis=0)
    return held.astype(F32)


def per_device(grads, weights, first, second, old_home, old_extra, new_home, new_extra):
    homes, width = weights.shape
    tiles = width // LANES
    outer = lax.axis_size("outer")
    devices = lax.axis_size("expert")
    tables = routes(homes, old_home, old_extra, new_home, new_extra)
    slot, source, extra_source, asked, moves, wants, adds, extra_adds = tables
    held = share_states(weights, first, second)
    mine = (lax.axis_index("expert") // plane_stride() % PLANE).astype(jnp.int32).reshape(1)
    per, _ = starts(tiles)
    head = 6 * per
    tail = -(-3 * tiles // 8) * 8
    heads = pl.pallas_call(
        states_kernel,
        in_specs=[SMEM] * 3 + [VMEM],
        out_specs=VMEM,
        out_shape=jax.ShapeDtypeStruct((devices, head, LANES), F32),
        scratch_shapes=[pltpu.VMEM((PLANE * homes, head, LANES), F32)] * 2,
        compiler_params=pltpu.CompilerParams(vmem_limit_bytes=16 * 2**20),
        cost_estimate=cost(1 << 18),
    )(mine, moves, wants, held)
    halves = split_by_core(grads, outer, width)
    pair = lax.all_to_all(halves, "core", 0, 0, tiled=True).astype(F32)
    partial = ((pair[0] + pair[1]) * PAIR_SCALE).astype(F16)
    parts = lax.all_to_all(partial, "outer", 0, 0, tiled=True)
    sums = jnp.sum(parts.astype(F32), axis=0) * (1.0 / PAIR_SCALE)
    outgoing = pl.pallas_call(
        sums_kernel,
        in_specs=[SMEM] * 2 + [VMEM] * 2,
        out_specs=VMEM,
        out_shape=jax.ShapeDtypeStruct((devices, head + tail, LANES), F32),
        scratch_shapes=[pltpu.VMEM((homes, tail, LANES), F32), pltpu.VMEM((tail, LANES), F32)],
        compiler_params=pltpu.CompilerParams(vmem_limit_bytes=16 * 2**20),
        cost_estimate=cost(1 << 18),
    )(slot, asked, sums, heads)
    arrived = lax.all_to_all(outgoing.astype(F16), "expert", 0, 0, tiled=True)
    extras = arrived[:, head : head + ROW, :].astype(F32)
    both = (source, extra_source)
    stride = plane_stride()
    planes = arrived.reshape(devices // (PLANE * stride), PLANE, stride, head + tail, LANES)
    size = (1, PLANE, 1, head, LANES)
    states = [lax.dynamic_slice(planes, (at // (PLANE * stride), 0, at % stride, 0, 0), size) for at in both]
    states = jnp.stack(states).reshape(2, PLANE, head, LANES)
    totals = jnp.concatenate([lax.dynamic_slice(arrived, (at, head, 0), (1, tail, LANES)) for at in both])
    states = states.astype(F32)
    totals = totals.astype(F32)
    return pl.pallas_call(
        final_kernel,
        in_specs=[SMEM] * 3 + [VMEM] * 7,
        out_specs=[VMEM] * 3,
        out_shape=[
            jax.ShapeDtypeStruct((homes + 1, width), BF16),
            jax.ShapeDtypeStruct((homes, width), F32),
            jax.ShapeDtypeStruct((homes, width), F32),
        ],
        scratch_shapes=[pltpu.VMEM((homes + 2, ROW, LANES), F32), pltpu.VMEM((3 * homes, width), F32)],
        compiler_params=pltpu.CompilerParams(vmem_limit_bytes=16 * 2**20),
        cost_estimate=cost(1 << 18),
    )(slot, adds, extra_adds, sums, extras, states, totals, weights, first, second)


def solution(mesh):
    groups, devices = mesh.devices.shape
    grid = Mesh(mesh.devices.reshape(groups // 2, 2, devices), ("outer", "core", "expert"))
    dp = ("outer", "core")
    placed = (P(dp, "expert", None), P("expert", dp), P("expert", dp), P("expert", dp), P(), P(), P(), P())
    return jax.shard_map(
        per_device,
        mesh=grid,
        in_specs=placed,
        out_specs=(P("expert", dp), P("expert", dp), P("expert", dp)),
        check_vma=False,
    )
```

```python
import jax
import jax.numpy as jnp
from jax import lax
from jax.experimental import pallas as pl
from jax.experimental.pallas import tpu as pltpu
from jax.sharding import Mesh
from jax.sharding import PartitionSpec as P

bias_first = 0.9999734386011124
bias_second = 0.994079470779696
LANES = 128
PLANE = 4
ORDER = (0, 2, 1, 3)
ROW = 16
PAIR_SCALE = 4096.0
SUM_SCALE = 256.0
STATE_SCALE = 16384.0

F32 = jnp.float32
F16 = jnp.float16
BF16 = jnp.bfloat16
VMEM = pl.BlockSpec(memory_space=pltpu.VMEM)
SMEM = pl.BlockSpec(memory_space=pltpu.SMEM)


def cost(n):
    return pl.CostEstimate(flops=n, bytes_accessed=4 * n, transcendentals=0)


def split_kernel(homes, width, steps, grads_ref, keep_ref, send_ref, line):
    tiles = width // LANES
    line[...] = jnp.zeros_like(line)
    core = lax.axis_index("core")
    for j in range(steps):
        for c, out_ref in ((core, keep_ref), (1 - core, send_ref)):
            at = pl.multiple_of((2 * j + c) * width, LANES)
            block = grads_ref[0, :, pl.ds(at, width)].astype(F32)
            for t in range(0, tiles, 2):
                low = block[:homes, t * LANES : (t + 1) * LANES]
                high = block[:homes, (t + 1) * LANES : (t + 2) * LANES]
                out_ref[j, t * homes : (t + 2) * homes, :] = jnp.concatenate([low, high], axis=0).astype(BF16)
            for t in range(tiles):
                line[t : t + 1, :] = block[homes : homes + 1, t * LANES : (t + 1) * LANES]
            out_ref[j, tiles * homes : tiles * homes + ROW, :] = line[...].astype(BF16)


def split_by_core(grads, outer, width):
    homes = grads.shape[1] - 1
    rows = (width // LANES) * homes + ROW
    steps = 4 if outer % 4 == 0 else 1
    return pl.pallas_call(
        lambda *refs: split_kernel(homes, width, steps, *refs),
        grid=(outer // steps,),
        in_specs=[pl.BlockSpec((1, homes + 1, steps * 2 * width), lambda i: (0, 0, i))],
        out_specs=[pl.BlockSpec((steps, rows, LANES), lambda i: (i, 0, 0))] * 2,
        out_shape=[jax.ShapeDtypeStruct((outer, rows, LANES), BF16)] * 2,
        scratch_shapes=[pltpu.VMEM((ROW, LANES), F32)],
        compiler_params=pltpu.CompilerParams(vmem_limit_bytes=16 * 2**20),
        cost_estimate=cost(1 << 19),
    )(grads)


def starts(tiles):
    per = -(-tiles // PLANE)
    return per, [min(y * per, tiles - per) for y in range(PLANE)]


def states_kernel(mine_ref, moves_ref, wants_ref, held_ref, out_ref, state_a, state_b):
    homes, width = held_ref.shape[2:]
    tiles = width // LANES
    per, _ = starts(tiles)
    mine = mine_ref[0]
    first_tile = jnp.minimum(mine * per, tiles - per)
    state_a[...] = jnp.zeros_like(state_a)
    state_b[...] = jnp.zeros_like(state_b)
    for r in range(PLANE):
        base = jnp.bitwise_xor(mine, ORDER[r]) * homes
        for n in range(3):
            for k in range(per):
                at = pl.multiple_of((first_tile + k) * LANES, LANES)
                value = held_ref[r, n, :, pl.ds(at, LANES)]
                for i in range(homes):
                    state_a[base + i, n * per + k : n * per + k + 1, :] = value[i : i + 1, :]
                    state_b[base + i, (3 + n) * per + k : (3 + n) * per + k + 1, :] = value[i : i + 1, :]
    for d in range(out_ref.shape[0]):
        out_ref[d] = state_a[moves_ref[d]] + state_b[wants_ref[d]]


def sums_kernel(slot_ref, asked_ref, sums_ref, heads_ref, out_ref, home, fixed):
    homes = home.shape[0]
    tiles = (sums_ref.shape[0] - ROW) // homes
    home[...] = jnp.zeros_like(home)
    fixed[...] = jnp.zeros_like(fixed)
    slot = slot_ref[0]
    for t in range(tiles):
        tile = sums_ref[t * homes : (t + 1) * homes, :] * SUM_SCALE
        row = 2 * tiles + t
        for i in range(homes):
            home[i, row : row + 1, :] = tile[i : i + 1, :]
        at = tiles * homes + t
        fixed[t : t + 1, :] = sums_ref[at : at + 1, :] * SUM_SCALE
    for t in range(tiles):
        row = 2 * tiles + t
        fixed[tiles + t : tiles + t + 1, :] = home[slot, row : row + 1, :]
    keep = fixed[...]
    head = heads_ref.shape[1]
    for d in range(out_ref.shape[0]):
        out_ref[d, :head, :] = heads_ref[d]
        out_ref[d, head:, :] = keep + home[asked_ref[d]]


def adam(total, base, first, second):
    moment1 = 0.9 * first + 0.1 * total
    moment2 = 0.95 * second + 0.05 * total * total
    step = moment1 / bias_first / (jnp.sqrt(moment2 / bias_second) + 1e-08)
    return base - 0.02 * (step + 0.1 * base), moment1, moment2


def final_kernel(
    slot_ref, adds_ref, extra_adds_ref, sums_ref, extras_ref, states_ref, totals_ref, w_ref, f_ref, s_ref, nw_ref, nf_ref, ns_ref, acc, flat
):
    homes, width = f_ref.shape
    tiles = width // LANES
    per, firsts = starts(tiles)
    slot = slot_ref[0]
    acc[...] = jnp.zeros_like(acc)
    copied = jnp.zeros(acc.shape[1:], F32)
    for s in range(extras_ref.shape[0]):
        acc[adds_ref[s]] += extras_ref[s]
        copied += extras_ref[s] * extra_adds_ref[s].astype(F32)
    acc[homes] = copied
    for y in range(PLANE):
        for k in range(per):
            cols = slice((firsts[y] + k) * LANES, (firsts[y] + k + 1) * LANES)
            for h in range(2):
                for n in range(3):
                    to = 2 * homes + 4 * h + n
                    at = (3 * h + n) * per + k
                    flat[to : to + 1, cols] = states_ref[h, y, at : at + 1, :]
    for t in range(tiles):
        cols = slice(t * LANES, (t + 1) * LANES)
        for i in range(homes + 1):
            flat[i : i + 1, cols] = acc[i, t : t + 1, :]
        for h in range(2):
            to = 2 * homes + 4 * h + 3
            at = (h + 1) * tiles + t
            flat[to : to + 1, cols] = totals_ref[h, at : at + 1, :]
    is_new = lax.broadcasted_iota(jnp.int32, (homes, LANES), 0) == slot
    for t in range(tiles):
        cols = slice(t * LANES, (t + 1) * LANES)
        got = flat[2 * homes : 2 * homes + 8, cols]
        own = sums_ref[t * homes : (t + 1) * homes, :]
        total = (flat[:homes, cols] + jnp.where(is_new, got[3:4], own * SUM_SCALE)) * (1.0 / SUM_SCALE)
        base = jnp.where(is_new, got[0:1] * (1.0 / STATE_SCALE), w_ref[:, cols].astype(F32))
        first = jnp.where(is_new, got[1:2] * (1.0 / STATE_SCALE), f_ref[:, cols])
        second = jnp.where(is_new, got[2:3] * (1.0 / STATE_SCALE), s_ref[:, cols])
        updated, moment1, moment2 = adam(total, base, first, second)
        total = (flat[homes : homes + 1, cols] + got[7:8]) * (1.0 / SUM_SCALE)
        state = got * (1.0 / STATE_SCALE)
        extra, _, _ = adam(total, state[4:5], state[5:6], state[6:7])
        nf_ref[:, cols] = moment1
        ns_ref[:, cols] = moment2
        nw_ref[:, cols] = jnp.concatenate([updated, extra], axis=0).astype(BF16)


def plane_stride():
    return max(lax.axis_size("expert") // 8, 1)


def routes(homes, old_home, old_extra, new_home, new_extra):
    me = lax.axis_index("expert")
    my_new = lax.dynamic_slice_in_dim(new_home, me * homes, homes)
    my_old = lax.dynamic_slice_in_dim(old_home, me * homes, homes)
    wanted = lax.dynamic_slice_in_dim(new_extra, me, 1)
    ids = jnp.arange(homes, dtype=jnp.int32)
    slot = jnp.sum(jnp.where(my_old != my_new, ids, 0)).reshape(1)
    places = jnp.arange(old_home.shape[0], dtype=jnp.int32)
    device = jnp.arange(new_extra.shape[0], dtype=jnp.int32)
    arrives = (old_home != new_home)[None, :] & (places[None, :] // homes == device[:, None])
    arriving = jnp.sum(jnp.where(arrives, new_home[None, :], 0), axis=1)
    moves = jnp.sum(jnp.where(arriving[:, None] == old_home[None, :], places[None, :], 0), axis=1)
    wants = jnp.sum(jnp.where(new_extra[:, None] == old_home[None, :], places[None, :], 0), axis=1)
    source = jnp.sum(jnp.where(device == me, moves // homes, 0))
    extra_source = jnp.sum(jnp.where(device == me, wants // homes, 0))
    asked = jnp.where(wants // homes == me, wants % homes, 0)
    spare = homes + 1
    adds = jnp.sum(jnp.where(old_extra[:, None] == my_new[None, :], ids[None, :] - spare, 0), axis=1) + spare
    extra_adds = (old_extra == wanted).astype(jnp.int32)
    stride = plane_stride()

    def in_plane(place):
        return (place // homes // stride) % PLANE * homes + place % homes

    return slot, source, extra_source, asked, in_plane(moves), in_plane(wants), adds, extra_adds


def share_states(weights, first, second):
    devices = lax.axis_size("expert")
    states = jnp.stack([weights.astype(F32), first, second])
    held = (states * STATE_SCALE).astype(F16)[None]
    for step in (2, 1):
        bit = step * plane_stride()
        other = lax.ppermute(held, "expert", [(i, i ^ bit) for i in range(devices)])
        held = jnp.concatenate([held, other], axis=0)
    return held.astype(F32)


def per_device(grads, weights, first, second, old_home, old_extra, new_home, new_extra):
    homes, width = weights.shape
    tiles = width // LANES
    outer = lax.axis_size("outer")
    devices = lax.axis_size("expert")
    tables = routes(homes, old_home, old_extra, new_home, new_extra)
    slot, source, extra_source, asked, moves, wants, adds, extra_adds = tables
    held = share_states(weights, first, second)
    mine = (lax.axis_index("expert") // plane_stride() % PLANE).astype(jnp.int32).reshape(1)
    per, _ = starts(tiles)
    head = 6 * per
    tail = -(-3 * tiles // 8) * 8
    heads = pl.pallas_call(
        states_kernel,
        in_specs=[SMEM] * 3 + [VMEM],
        out_specs=VMEM,
        out_shape=jax.ShapeDtypeStruct((devices, head, LANES), F32),
        scratch_shapes=[pltpu.VMEM((PLANE * homes, head, LANES), F32)] * 2,
        compiler_params=pltpu.CompilerParams(vmem_limit_bytes=16 * 2**20),
        cost_estimate=cost(1 << 18),
    )(mine, moves, wants, held)
    kept, sent = split_by_core(grads, outer, width)
    other = lax.ppermute(sent, "core", [(0, 1), (1, 0)])
    partial = ((kept.astype(F32) + other.astype(F32)) * PAIR_SCALE).astype(F16)
    parts = lax.all_to_all(partial, "outer", 0, 0, tiled=True)
    sums = jnp.sum(parts.astype(F32), axis=0) * (1.0 / PAIR_SCALE)
    outgoing = pl.pallas_call(
        sums_kernel,
        in_specs=[SMEM] * 2 + [VMEM] * 2,
        out_specs=VMEM,
        out_shape=jax.ShapeDtypeStruct((devices, head + tail, LANES), F32),
        scratch_shapes=[pltpu.VMEM((homes, tail, LANES), F32), pltpu.VMEM((tail, LANES), F32)],
        compiler_params=pltpu.CompilerParams(vmem_limit_bytes=16 * 2**20),
        cost_estimate=cost(1 << 18),
    )(slot, asked, sums, heads)
    arrived = lax.all_to_all(outgoing.astype(F16), "expert", 0, 0, tiled=True)
    extras = arrived[:, head : head + ROW, :].astype(F32)
    both = (source, extra_source)
    stride = plane_stride()
    planes = arrived.reshape(devices // (PLANE * stride), PLANE, stride, head + tail, LANES)
    size = (1, PLANE, 1, head, LANES)
    states = [lax.dynamic_slice(planes, (at // (PLANE * stride), 0, at % stride, 0, 0), size) for at in both]
    states = jnp.stack(states).reshape(2, PLANE, head, LANES)
    totals = jnp.concatenate([lax.dynamic_slice(arrived, (at, head, 0), (1, tail, LANES)) for at in both])
    states = states.astype(F32)
    totals = totals.astype(F32)
    return pl.pallas_call(
        final_kernel,
        in_specs=[SMEM] * 3 + [VMEM] * 7,
        out_specs=[VMEM] * 3,
        out_shape=[
            jax.ShapeDtypeStruct((homes + 1, width), BF16),
            jax.ShapeDtypeStruct((homes, width), F32),
            jax.ShapeDtypeStruct((homes, width), F32),
        ],
        scratch_shapes=[pltpu.VMEM((homes + 2, ROW, LANES), F32), pltpu.VMEM((3 * homes, width), F32)],
        compiler_params=pltpu.CompilerParams(vmem_limit_bytes=16 * 2**20),
        cost_estimate=cost(1 << 18),
    )(slot, adds, extra_adds, sums, extras, states, totals, weights, first, second)


def solution(mesh):
    groups, devices = mesh.devices.shape
    grid = Mesh(mesh.devices.reshape(groups // 2, 2, devices), ("outer", "core", "expert"))
    dp = ("outer", "core")
    placed = (P(dp, "expert", None), P("expert", dp), P("expert", dp), P("expert", dp), P(), P(), P(), P())
    return jax.shard_map(
        per_device,
        mesh=grid,
        in_specs=placed,
        out_specs=(P("expert", dp), P("expert", dp), P("expert", dp)),
        check_vma=False,
    )
```

```python
import jax
import jax.numpy as jnp
from jax import lax
from jax.experimental import pallas as pl
from jax.experimental.pallas import tpu as pltpu
from jax.sharding import Mesh
from jax.sharding import PartitionSpec as P

bias_first = 0.9999734386011124
bias_second = 0.994079470779696
LANES = 128
PLANE = 4
ORDER = (0, 2, 1, 3)
ROW = 16
PAIR_SCALE = 4096.0
SUM_SCALE = 256.0
STATE_SCALE = 16384.0

F32 = jnp.float32
F16 = jnp.float16
BF16 = jnp.bfloat16
VMEM = pl.BlockSpec(memory_space=pltpu.VMEM)
SMEM = pl.BlockSpec(memory_space=pltpu.SMEM)


def cost(n):
    return pl.CostEstimate(flops=n, bytes_accessed=4 * n, transcendentals=0)


def split_kernel(homes, width, steps, grads_ref, out_ref, line):
    tiles = width // LANES
    line[...] = jnp.zeros_like(line)
    for j in range(steps):
        for c in range(2):
            at = (2 * j + c) * width
            block = grads_ref[0, :, at : at + width].astype(F32)
            for t in range(0, tiles, 2):
                low = block[:homes, t * LANES : (t + 1) * LANES]
                high = block[:homes, (t + 1) * LANES : (t + 2) * LANES]
                out_ref[c, j, t * homes : (t + 2) * homes, :] = jnp.concatenate([low, high], axis=0).astype(BF16)
            for t in range(tiles):
                line[t : t + 1, :] = block[homes : homes + 1, t * LANES : (t + 1) * LANES]
            out_ref[c, j, tiles * homes : tiles * homes + ROW, :] = line[...].astype(BF16)


def split_by_core(grads, outer, width):
    homes = grads.shape[1] - 1
    rows = (width // LANES) * homes + ROW
    steps = 4 if outer % 4 == 0 else 1
    return pl.pallas_call(
        lambda *refs: split_kernel(homes, width, steps, *refs),
        grid=(outer // steps,),
        in_specs=[pl.BlockSpec((1, homes + 1, steps * 2 * width), lambda i: (0, 0, i))],
        out_specs=pl.BlockSpec((2, steps, rows, LANES), lambda i: (0, i, 0, 0)),
        out_shape=jax.ShapeDtypeStruct((2, outer, rows, LANES), BF16),
        scratch_shapes=[pltpu.VMEM((ROW, LANES), F32)],
        cost_estimate=cost(1 << 19),
    )(grads)


def starts(tiles):
    per = -(-tiles // PLANE)
    return per, [min(y * per, tiles - per) for y in range(PLANE)]


def states_kernel(mine_ref, moves_ref, wants_ref, held_ref, out_ref, state_a, state_b):
    homes, width = held_ref.shape[2:]
    tiles = width // LANES
    per, _ = starts(tiles)
    mine = mine_ref[0]
    first_tile = jnp.minimum(mine * per, tiles - per)
    state_a[...] = jnp.zeros_like(state_a)
    state_b[...] = jnp.zeros_like(state_b)
    for r in range(PLANE):
        base = jnp.bitwise_xor(mine, ORDER[r]) * homes
        for n in range(3):
            for k in range(per):
                at = pl.multiple_of((first_tile + k) * LANES, LANES)
                value = held_ref[r, n, :, pl.ds(at, LANES)]
                for i in range(homes):
                    state_a[base + i, n * per + k : n * per + k + 1, :] = value[i : i + 1, :]
                    state_b[base + i, (3 + n) * per + k : (3 + n) * per + k + 1, :] = value[i : i + 1, :]
    for d in range(out_ref.shape[0]):
        out_ref[d] = state_a[moves_ref[d]] + state_b[wants_ref[d]]


def sums_kernel(slot_ref, asked_ref, sums_ref, heads_ref, out_ref, home, fixed):
    homes = home.shape[0]
    tiles = (sums_ref.shape[0] - ROW) // homes
    home[...] = jnp.zeros_like(home)
    fixed[...] = jnp.zeros_like(fixed)
    slot = slot_ref[0]
    for t in range(tiles):
        tile = sums_ref[t * homes : (t + 1) * homes, :] * SUM_SCALE
        row = 2 * tiles + t
        for i in range(homes):
            home[i, row : row + 1, :] = tile[i : i + 1, :]
        at = tiles * homes + t
        fixed[t : t + 1, :] = sums_ref[at : at + 1, :] * SUM_SCALE
    for t in range(tiles):
        row = 2 * tiles + t
        fixed[tiles + t : tiles + t + 1, :] = home[slot, row : row + 1, :]
    keep = fixed[...]
    head = heads_ref.shape[1]
    for d in range(out_ref.shape[0]):
        out_ref[d, :head, :] = heads_ref[d]
        out_ref[d, head:, :] = keep + home[asked_ref[d]]


def adam(total, base, first, second):
    moment1 = 0.9 * first + 0.1 * total
    moment2 = 0.95 * second + 0.05 * total * total
    step = moment1 / bias_first / (jnp.sqrt(moment2 / bias_second) + 1e-08)
    return base - 0.02 * (step + 0.1 * base), moment1, moment2


def final_kernel(
    slot_ref, adds_ref, extra_adds_ref, sums_ref, extras_ref, states_ref, totals_ref, w_ref, f_ref, s_ref, nw_ref, nf_ref, ns_ref, acc, flat
):
    homes, width = f_ref.shape
    tiles = width // LANES
    per, firsts = starts(tiles)
    slot = slot_ref[0]
    acc[...] = jnp.zeros_like(acc)
    copied = jnp.zeros(acc.shape[1:], F32)
    for s in range(extras_ref.shape[0]):
        acc[adds_ref[s]] += extras_ref[s]
        copied += extras_ref[s] * extra_adds_ref[s].astype(F32)
    acc[homes] = copied
    for y in range(PLANE):
        for k in range(per):
            cols = slice((firsts[y] + k) * LANES, (firsts[y] + k + 1) * LANES)
            for h in range(2):
                for n in range(3):
                    to = 2 * homes + 4 * h + n
                    at = (3 * h + n) * per + k
                    flat[to : to + 1, cols] = states_ref[h, y, at : at + 1, :]
    for t in range(tiles):
        cols = slice(t * LANES, (t + 1) * LANES)
        for i in range(homes + 1):
            flat[i : i + 1, cols] = acc[i, t : t + 1, :]
        for h in range(2):
            to = 2 * homes + 4 * h + 3
            at = (h + 1) * tiles + t
            flat[to : to + 1, cols] = totals_ref[h, at : at + 1, :]
    is_new = lax.broadcasted_iota(jnp.int32, (homes, LANES), 0) == slot
    for t in range(tiles):
        cols = slice(t * LANES, (t + 1) * LANES)
        got = flat[2 * homes : 2 * homes + 8, cols]
        own = sums_ref[t * homes : (t + 1) * homes, :]
        total = (flat[:homes, cols] + jnp.where(is_new, got[3:4], own * SUM_SCALE)) * (1.0 / SUM_SCALE)
        base = jnp.where(is_new, got[0:1] * (1.0 / STATE_SCALE), w_ref[:, cols].astype(F32))
        first = jnp.where(is_new, got[1:2] * (1.0 / STATE_SCALE), f_ref[:, cols])
        second = jnp.where(is_new, got[2:3] * (1.0 / STATE_SCALE), s_ref[:, cols])
        updated, moment1, moment2 = adam(total, base, first, second)
        total = (flat[homes : homes + 1, cols] + got[7:8]) * (1.0 / SUM_SCALE)
        state = got * (1.0 / STATE_SCALE)
        extra, _, _ = adam(total, state[4:5], state[5:6], state[6:7])
        nf_ref[:, cols] = moment1
        ns_ref[:, cols] = moment2
        nw_ref[:, cols] = jnp.concatenate([updated, extra], axis=0).astype(BF16)


def plane_stride():
    return max(lax.axis_size("expert") // 8, 1)


def routes(homes, old_home, old_extra, new_home, new_extra):
    me = lax.axis_index("expert")
    my_new = lax.dynamic_slice_in_dim(new_home, me * homes, homes)
    my_old = lax.dynamic_slice_in_dim(old_home, me * homes, homes)
    wanted = lax.dynamic_slice_in_dim(new_extra, me, 1)
    ids = jnp.arange(homes, dtype=jnp.int32)
    slot = jnp.sum(jnp.where(my_old != my_new, ids, 0)).reshape(1)
    places = jnp.arange(old_home.shape[0], dtype=jnp.int32)
    device = jnp.arange(new_extra.shape[0], dtype=jnp.int32)
    arrives = (old_home != new_home)[None, :] & (places[None, :] // homes == device[:, None])
    arriving = jnp.sum(jnp.where(arrives, new_home[None, :], 0), axis=1)
    moves = jnp.sum(jnp.where(arriving[:, None] == old_home[None, :], places[None, :], 0), axis=1)
    wants = jnp.sum(jnp.where(new_extra[:, None] == old_home[None, :], places[None, :], 0), axis=1)
    source = jnp.sum(jnp.where(device == me, moves // homes, 0))
    extra_source = jnp.sum(jnp.where(device == me, wants // homes, 0))
    asked = jnp.where(wants // homes == me, wants % homes, 0)
    spare = homes + 1
    adds = jnp.sum(jnp.where(old_extra[:, None] == my_new[None, :], ids[None, :] - spare, 0), axis=1) + spare
    extra_adds = (old_extra == wanted).astype(jnp.int32)
    stride = plane_stride()

    def in_plane(place):
        return (place // homes // stride) % PLANE * homes + place % homes

    return slot, source, extra_source, asked, in_plane(moves), in_plane(wants), adds, extra_adds


def share_states(weights, first, second):
    devices = lax.axis_size("expert")
    states = jnp.stack([weights.astype(F32), first, second])
    held = (states * STATE_SCALE).astype(F16)[None]
    for step in (2, 1):
        bit = step * plane_stride()
        other = lax.ppermute(held, "expert", [(i, i ^ bit) for i in range(devices)])
        held = jnp.concatenate([held, other], axis=0)
    return held.astype(F32)


def per_device(grads, weights, first, second, old_home, old_extra, new_home, new_extra):
    homes, width = weights.shape
    tiles = width // LANES
    outer = lax.axis_size("outer")
    devices = lax.axis_size("expert")
    tables = routes(homes, old_home, old_extra, new_home, new_extra)
    slot, source, extra_source, asked, moves, wants, adds, extra_adds = tables
    held = share_states(weights, first, second)
    mine = (lax.axis_index("expert") // plane_stride() % PLANE).astype(jnp.int32).reshape(1)
    per, _ = starts(tiles)
    head = 6 * per
    tail = -(-3 * tiles // 8) * 8
    heads = pl.pallas_call(
        states_kernel,
        in_specs=[SMEM] * 3 + [VMEM],
        out_specs=VMEM,
        out_shape=jax.ShapeDtypeStruct((devices, head, LANES), F32),
        scratch_shapes=[pltpu.VMEM((PLANE * homes, head, LANES), F32)] * 2,
        compiler_params=pltpu.CompilerParams(vmem_limit_bytes=16 * 2**20),
        cost_estimate=cost(1 << 18),
    )(mine, moves, wants, held)
    halves = split_by_core(grads, outer, width)
    pair = lax.all_to_all(halves, "core", 0, 0, tiled=True).astype(F32)
    partial = ((pair[0] + pair[1]) * PAIR_SCALE).astype(F16)
    parts = lax.all_to_all(partial, "outer", 0, 0, tiled=True)
    sums = jnp.sum(parts.astype(F32), axis=0) * (1.0 / PAIR_SCALE)
    outgoing = pl.pallas_call(
        sums_kernel,
        in_specs=[SMEM] * 2 + [VMEM] * 2,
        out_specs=VMEM,
        out_shape=jax.ShapeDtypeStruct((devices, head + tail, LANES), F32),
        scratch_shapes=[pltpu.VMEM((homes, tail, LANES), F32), pltpu.VMEM((tail, LANES), F32)],
        compiler_params=pltpu.CompilerParams(vmem_limit_bytes=16 * 2**20),
        cost_estimate=cost(1 << 18),
    )(slot, asked, sums, heads)
    arrived = lax.all_to_all(outgoing.astype(F16), "expert", 0, 0, tiled=True)
    extras = arrived[:, head : head + ROW, :].astype(F32)
    both = (source, extra_source)
    stride = plane_stride()
    planes = arrived.reshape(devices // (PLANE * stride), PLANE, stride, head + tail, LANES)
    size = (1, PLANE, 1, head, LANES)
    states = [lax.dynamic_slice(planes, (at // (PLANE * stride), 0, at % stride, 0, 0), size) for at in both]
    states = jnp.stack(states).reshape(2, PLANE, head, LANES)
    totals = jnp.concatenate([lax.dynamic_slice(arrived, (at, head, 0), (1, tail, LANES)) for at in both])
    states = states.astype(F32)
    totals = totals.astype(F32)
    return pl.pallas_call(
        final_kernel,
        in_specs=[SMEM] * 3 + [VMEM] * 7,
        out_specs=[VMEM] * 3,
        out_shape=[
            jax.ShapeDtypeStruct((homes + 1, width), BF16),
            jax.ShapeDtypeStruct((homes, width), F32),
            jax.ShapeDtypeStruct((homes, width), F32),
        ],
        scratch_shapes=[pltpu.VMEM((homes + 2, ROW, LANES), F32), pltpu.VMEM((3 * homes, width), F32)],
        compiler_params=pltpu.CompilerParams(vmem_limit_bytes=16 * 2**20),
        cost_estimate=cost(1 << 18),
    )(slot, adds, extra_adds, sums, extras, states, totals, weights, first, second)


def solution(mesh):
    groups, devices = mesh.devices.shape
    grid = Mesh(mesh.devices.reshape(groups // 2, 2, devices), ("outer", "core", "expert"))
    dp = ("outer", "core")
    placed = (P(dp, "expert", None), P("expert", dp), P("expert", dp), P("expert", dp), P(), P(), P(), P())
    return jax.shard_map(
        per_device,
        mesh=grid,
        in_specs=placed,
        out_specs=(P("expert", dp), P("expert", dp), P("expert", dp)),
        check_vma=False,
    )
```
